512 devices in a mesh: dp: 64 (over z, x), cuts: 8 (over y, core).
Axes of the slice: x: 4, y: 4, z: 16, core: 2. Of those that a mesh axis runs over, the one named last changes fastest.
Arguments:
- queries: bfloat16 [512, 2048], P('dp', 'cuts'), may hold values from -240 to 240
- new_keys: bfloat16 [512, 2048], P('dp', 'cuts'), may hold values from -6 to 6
- new_values: bfloat16 [512, 2048], P('dp', 'cuts'), may hold values from -6 to 6
- key_cache: bfloat16 [512, 64, 2048], P('dp', None, 'cuts'), may hold values from -6 to 6
- value_cache: bfloat16 [512, 64, 2048], P('dp', None, 'cuts'), may hold values from -6 to 6
- lengths: int32 [512], P('dp'), may hold values from 1 to 64
- resid: bfloat16 [512, 2048], P('dp'), may hold values from -6 to 6
- norm_gain: float32 [2048], replicated, may hold values from 0.5 to 1.5
- w_out: bfloat16 [2048, 2048], P('cuts'), may hold values from -0.125 to 0.125
- experts: int32 [512, 1], P('dp'), may hold values from 0 to 15; in each aligned block of 8 rows (0 to 7, 8 to 15, ...) at most 2 rows name the same one
- w_up: bfloat16 [64, 2048, 2048], P('dp', None, 'cuts'), may hold values from -0.125 to 0.125
- w_down: bfloat16 [64, 2048, 2048], P('dp', 'cuts'), may hold values from -0.0625 to 0.0625
Outputs:
- mixed: bfloat16 [512, 2048], P('dp', 'cuts')
The draws below stay inside these ranges and needn't reach their ends.
Inputs may be any that keep to these rules, and one draw needn't show every extreme that they name: `experts`: among the 8 rows of one dp index each expert is named by at most 2 rows, and by exactly 2 in some.
All inputs are finite; a program needn't handle non-finite values.
Results may differ from the reference program's by a relative error of at most 0.014.
Values may be sent and summed in bfloat16 or wider, within the bound.
No kernel may reach another device: no remote copies, remote signals or barrier semaphores. Data moves between devices by JAX's collectives and lax.ppermute only.
A program may use at most 64 MiB of HBM per device.

```python
import math
import jax
import jax.numpy as jnp
import numpy as np
from jax import lax

D = 2048
HEADS = 16
HD = 128
FF = 8192
GROUP = 4
ROWS = 8
LEN = 64
EXPERTS = 16
CAP = 2
TOKENS = 512
N_DP = 64
N_CUTS = 8


def draw_queries(key, part):
    key = jax.random.fold_in(key, 11)
    base = jax.random.truncated_normal(key, -6.0, 6.0, (TOKENS, HEADS * HD), jnp.float32)
    return base.astype(jnp.bfloat16)


def place_ends(values, stream_key, smallest, high):
    dims = values.shape
    place = [jax.random.randint(jax.random.fold_in(stream_key, axis), (), 0, dims[axis]) for axis in range(len(dims))]
    values = values.at[tuple(place)].set(smallest)
    longest = dims.index(max(dims))
    place[longest] = (place[longest] + 1) % dims[longest]
    return values.at[tuple(place)].set(high)


def block_levels(stream_key, shape, cuts, least, largest):
    factor_of = 1.0
    for dim, shards_of in cuts:
        steps = jax.random.uniform(jax.random.fold_in(jax.random.fold_in(stream_key, 6), dim), (shards_of,), jnp.float32, least / len(cuts), largest / len(cuts))
        factor_of = factor_of * jnp.repeat(jnp.exp(steps), shape[dim] // shards_of).reshape((-1,) + (1,) * (len(shape) - 1 - dim))
    return factor_of


def deal_out(stream_key, own, number, rows, number_of, top, bound, slope):
    sequence = jax.random.permutation(stream_key, number_of)
    packed, usual = load_shares(number_of, rows * top, bound, slope, True), load_shares(number_of, rows * top, bound, slope, False)
    places = jnp.arange(number_of)

    def named(tallies, offset_by):
        used = int((tallies > 0).sum())
        fixed = max(1, used // 4)
        passed = fixed + (places - fixed + offset_by * (used - fixed)) % max(1, number_of - fixed)
        return jnp.zeros((number_of,), jnp.int32).at[sequence[jnp.where(places < fixed, places, passed)]].set(jnp.asarray(tallies, jnp.int32))

    tallies = jnp.where(number % 4 == 0, named(packed, number // 4), named(usual, number - number // 4 - 1))
    mixed = jax.random.permutation(jax.random.fold_in(own, 3), number_of)
    giver, sink = mixed[0:number_of // 2 * 2:2], mixed[1:number_of // 2 * 2:2]
    margin = jnp.minimum(tallies[giver] - 1, bound - tallies[sink]) // 2
    margin = jnp.where((giver == sequence[0]) | (sink == sequence[0]) | (tallies[sink] == 0), 0, jnp.maximum(margin, 0))
    passed = jax.random.randint(jax.random.fold_in(own, 4), (number_of // 2,), 0, 1 << 20) % (margin + 1)
    tallies = tallies.at[giver].add(-passed).at[sink].add(passed)
    members = jnp.searchsorted(jnp.cumsum(tallies), jnp.arange(rows * top), side="right").astype(jnp.int32)
    table = members.reshape(top, rows).T
    table = table[jax.random.permutation(jax.random.fold_in(own, 1), rows)]
    offset_by = jax.random.randint(jax.random.fold_in(own, 2), (rows, 1), 0, top)
    return jnp.take_along_axis(table, (jnp.arange(top)[None, :] + offset_by) % top, axis=1)


def load_shares(number_of, total, reach, slope, full):
    loads = [(1 << 20) // math.isqrt(standing ** slope) + 1 for standing in range(1, number_of + 1)]
    largest = reach if full else min(reach, max(-(-total // number_of), total * loads[0] // sum(loads)))
    least = 1 if total - largest >= number_of - 1 else 0
    holding, spare = [largest] + [least] * (number_of - 1), total - largest - least * (number_of - 1)
    while spare > 0:
        movable = [i for i in range(1, number_of) if holding[i] < largest] or [i for i in range(1, number_of) if holding[i] < reach]
        whole, remaining = sum([loads[i] for i in movable]), spare
        for i in movable:
            addition = min(reach - holding[i], max(1, remaining * loads[i] // whole), spare)
            holding[i] = holding[i] + addition
            spare = spare - addition
    return np.array(holding)


def scatter_about(rng, shape, deviation, limit, shards=(), kind=jnp.bfloat16):
    values = jax.random.normal(rng, shape, jnp.float32) * deviation
    if len(shards) > 0:
        values = block_levels(rng, shape, shards, -0.22, 0.18) * values
    return jnp.clip(values, min=-limit, max=limit).astype(kind)


def setup_inputs(seed: int = 0) -> dict:
    key_list = jax.random.split(jax.random.key(seed), 13)
    queries = draw_queries(jax.random.fold_in(key_list[12], 71), 0)
    new_keys = scatter_about(key_list[1], (TOKENS, HEADS * HD), 1.0, 6.0, ((0, 64), (1, 8)))
    new_values = scatter_about(key_list[2], (TOKENS, HEADS * HD), 1.0, 6.0, ((0, 64), (1, 8)))
    key_cache = scatter_about(key_list[3], (TOKENS, LEN, HEADS * HD), 1.0, 6.0, ((0, 64), (2, 8)))
    value_cache = scatter_about(key_list[4], (TOKENS, LEN, HEADS * HD), 1.0, 6.0, ((0, 64), (2, 8)))
    lengths = place_ends(jax.random.randint(key_list[5], (TOKENS,), 1, LEN + 1), jax.random.fold_in(key_list[5], 1), 1, LEN).astype(jnp.int32)
    resid = scatter_about(key_list[6], (TOKENS, D), 1.0, 6.0, ((0, 64),))
    norm_gain = jnp.clip(1.0 + 0.1 * jax.random.normal(key_list[7], (D,), jnp.float32), 0.5, 1.5)
    w_out = scatter_about(key_list[8], (HEADS * HD, D), (HEADS * HD) ** -0.5, 0.125, ((0, 8),))
    experts_keys = jax.random.split(jax.random.fold_in(key_list[9], 1), TOKENS // ROWS)
    experts_turns = jax.random.permutation(jax.random.fold_in(key_list[9], 3), TOKENS // ROWS)
    experts = jax.vmap(lambda own, number: deal_out(jax.random.fold_in(key_list[9], 2), own, number, ROWS, EXPERTS, 1, CAP, 2))(experts_keys, experts_turns).reshape((TOKENS, 1))
    w_up = scatter_about(key_list[10], (EXPERTS * GROUP, D, FF // GROUP), D ** -0.5, 0.125, ((0, 64), (2, 8)))
    w_down = scatter_about(key_list[11], (EXPERTS * GROUP, FF // GROUP, D), FF ** -0.5, 0.0625, ((0, 64), (1, 8)))
    return dict(queries=queries, new_keys=new_keys, new_values=new_values, key_cache=key_cache, value_cache=value_cache, lengths=lengths, resid=resid, norm_gain=norm_gain, w_out=w_out, experts=experts, w_up=w_up, w_down=w_down)


def attend(block):
    query, nkey, nval, kcache, vcache, valid_len = block
    count = query.shape[0]
    scale = 1.0 / HD ** 0.5
    qf = query.astype(jnp.float32).reshape(count, HEADS, HD)
    kf = kcache.astype(jnp.float32).reshape(count, LEN, HEADS, HD)
    vf = vcache.astype(jnp.float32).reshape(count, LEN, HEADS, HD)
    nk = nkey.astype(jnp.float32).reshape(count, HEADS, HD)
    nv = nval.astype(jnp.float32).reshape(count, HEADS, HD)
    scores = jnp.einsum('rhd,rjhd->rhj', qf, kf) * scale
    keep = jnp.arange(LEN)[None, None, :] < valid_len[:, None, None]
    scores = jnp.where(keep, scores, -1e+30)
    fresh = lax.optimization_barrier(jnp.sum(qf * nk, axis=-1)) * scale
    peak = jnp.maximum(lax.optimization_barrier(jnp.max(scores, axis=-1)), fresh)
    pcache = jnp.where(keep, jnp.exp(scores - peak[..., None]), 0.0)
    pnew = jnp.exp(fresh - peak)
    total = lax.optimization_barrier(jnp.sum(pcache, axis=-1)) + pnew
    pcache = (pcache / total[..., None]).astype(jnp.bfloat16)
    pnew = (pnew / total).astype(jnp.bfloat16)
    summed = jnp.einsum('rhj,rjhd->rhd', pcache.astype(jnp.float32), vf)
    summed = summed + pnew.astype(jnp.float32)[..., None] * nv
    return summed.reshape(count, HEADS * HD).astype(jnp.bfloat16)

def reference(queries, new_keys, new_values, key_cache, value_cache, lengths, resid, norm_gain, w_out, experts, w_up, w_down):
    blocks = (queries.reshape(N_DP, ROWS, HEADS * HD), new_keys.reshape(N_DP, ROWS, HEADS * HD), new_values.reshape(N_DP, ROWS, HEADS * HD), key_cache.reshape(N_DP, ROWS, LEN, HEADS * HD), value_cache.reshape(N_DP, ROWS, LEN, HEADS * HD), lengths.reshape(N_DP, ROWS))
    heads_out = lax.map(attend, blocks).reshape(TOKENS, HEADS * HD)
    attn = jnp.dot(heads_out, w_out, preferred_element_type=jnp.float32)
    hidden = resid.astype(jnp.float32) + attn
    meansq = lax.optimization_barrier(jnp.mean(hidden * hidden, axis=-1))
    normed = (hidden * lax.rsqrt(meansq + 1e-06)[:, None] * norm_gain[None, :]).astype(jnp.bfloat16)
    ids = experts[:, 0]
    slots_all = CAP * N_DP
    block_units = FF // GROUP // N_CUTS

    def one_expert(carry, expert):
        order = jnp.argsort((ids != expert).astype(jnp.int32), stable=True)[:slots_all].astype(jnp.int32)
        chosen = ids[order] == expert
        picked = normed[order]
        total = jnp.zeros((slots_all, D), jnp.float32)
        for group_idx in range(GROUP):
            upper = w_up[expert * GROUP + group_idx]
            lower = w_down[expert * GROUP + group_idx]
            act = jax.nn.gelu(jnp.dot(picked, upper, preferred_element_type=jnp.float32)).astype(jnp.bfloat16)
            part = jnp.zeros((slots_all, D), jnp.float32)
            for cut_idx in range(N_CUTS):
                lo_unit = cut_idx * block_units
                piece = jnp.dot(act[:, lo_unit:lo_unit + block_units], lower[lo_unit:lo_unit + block_units], preferred_element_type=jnp.float32).astype(jnp.bfloat16)
                part = part + lax.optimization_barrier(piece).astype(jnp.float32)
            rounded = lax.optimization_barrier(part.astype(jnp.bfloat16))
            total = total + rounded.astype(jnp.float32)
        carry = carry.at[order].add(jnp.where(chosen[:, None], total, 0.0))
        return (carry, None)
    expert_out, unused = lax.scan(one_expert, jnp.zeros((TOKENS, D), jnp.float32), jnp.arange(EXPERTS, dtype=jnp.int32))
    return (hidden + expert_out).astype(jnp.bfloat16)
```

```python
import jax
import jax.numpy as jnp
from jax import lax
from jax.sharding import Mesh
from jax.sharding import PartitionSpec as P

HD = 128
GROUP = 4
CORES = 2
SLOTS = 2


def attend_local(queries, new_keys, new_values, key_cache, value_cache, lengths):
    count, feats = queries.shape
    heads = feats // HD
    length = key_cache.shape[1]
    scale = 1.0 / HD**0.5
    query = queries.reshape(count, heads, HD)
    kcache = key_cache.reshape(count, length, heads, HD)
    vcache = value_cache.reshape(count, length, heads, HD)
    nkey = new_keys.reshape(count, heads, HD)
    nval = new_values.reshape(count, heads, HD)
    scores = jnp.einsum("rhd,rjhd->rhj", query, kcache, preferred_element_type=jnp.float32) * scale
    keep = jnp.arange(length)[None, None, :] < lengths[:, None, None]
    scores = jnp.where(keep, scores, -1e30)
    fresh = jnp.einsum("rhd,rhd->rh", query, nkey, preferred_element_type=jnp.float32) * scale
    peak = jnp.maximum(jnp.max(scores, axis=-1), fresh)
    pcache = jnp.where(keep, jnp.exp(scores - peak[..., None]), 0.0)
    pnew = jnp.exp(fresh - peak)
    total = jnp.sum(pcache, axis=-1) + pnew
    pcache = (pcache / total[..., None]).astype(jnp.bfloat16)
    pnew = (pnew / total).astype(jnp.bfloat16)
    summed = jnp.einsum("rhj,rjhd->rhd", pcache, vcache, preferred_element_type=jnp.float32)
    summed = summed + pnew.astype(jnp.float32)[..., None] * nval.astype(jnp.float32)
    return summed.reshape(count, feats).astype(jnp.bfloat16)


def on_device(
    queries,
    new_keys,
    new_values,
    key_cache,
    value_cache,
    lengths,
    resid,
    norm_gain,
    w_out,
    experts,
    w_up,
    w_down,
):
    bf16, f32 = jnp.bfloat16, jnp.float32
    count, width_all = resid.shape
    n_z, n_x, n_y = lax.axis_size("z"), lax.axis_size("x"), lax.axis_size("y")
    width = width_all // (n_y * CORES)
    core = lax.axis_index("core")
    my_y = lax.axis_index("y")

    heads_out = attend_local(queries, new_keys, new_values, key_cache, value_cache, lengths)
    partial = jnp.dot(heads_out, w_out, preferred_element_type=f32)
    both = lax.all_gather(partial, "core", axis=0)

    ids = experts[:, 0]
    order_idx = jnp.arange(count, dtype=jnp.int32)
    earlier = (ids[:, None] == ids[None, :]) & (order_idx[:, None] > order_idx[None, :])
    slot_id = ids * SLOTS + jnp.sum(earlier.astype(jnp.int32), axis=1)
    table = jnp.arange(n_z * SLOTS, dtype=jnp.int32)[:, None] == slot_id[None, :]

    def own_half(a):
        split = a.reshape(a.shape[:-1] + (n_y, CORES, width))
        return lax.dynamic_index_in_dim(split, core, split.ndim - 2, keepdims=False)

    chip = own_half(both[0] + both[1])
    rest = own_half(resid).astype(f32)
    mine = (jnp.arange(n_y) == my_y)[None, :, None]
    chip = (chip + jnp.where(mine, rest, 0.0)).astype(bf16)
    packed = jnp.einsum("sr,ryc->syc", table.astype(bf16), chip, preferred_element_type=f32)
    packed = packed.astype(bf16).reshape(n_z, SLOTS, n_y, width).transpose(0, 2, 1, 3)
    packed = packed.reshape(n_z * n_y, SLOTS, width)
    got = lax.all_to_all(packed, ("z", "y"), split_axis=0, concat_axis=0, tiled=True)
    slots = n_z * SLOTS
    hidden = jnp.sum(got.reshape(n_z, n_y, SLOTS, width).astype(f32), axis=1).reshape(slots, width)

    spread = jnp.broadcast_to(hidden.astype(bf16)[None], (n_x * n_y, slots, width))
    plane = lax.all_to_all(spread, ("x", "y"), split_axis=0, concat_axis=0, tiled=True)
    pair = lax.all_gather(plane, "core", axis=0)
    rows = pair.reshape(CORES, n_x, n_y, slots, width).transpose(1, 3, 2, 0, 4)
    rows = rows.reshape(n_x * slots, width_all).astype(f32)
    meansq = jnp.mean(rows * rows, axis=-1)
    normed = (rows * lax.rsqrt(meansq + 1e-06)[:, None] * norm_gain[None, :]).astype(bf16)
    act = jax.nn.gelu(jnp.dot(normed, w_up[0], preferred_element_type=f32)).astype(bf16)
    piece = jnp.dot(act, w_down[0], preferred_element_type=f32).astype(bf16)
    pieces = lax.all_gather(piece, "core", axis=0)
    half = own_half(pieces).astype(f32)
    half = (half[0] + half[1]).astype(bf16)
    half = half.reshape(n_x, slots, n_y, width).transpose(0, 2, 1, 3)
    half = half.reshape(n_x * n_y, slots, width)
    parts = lax.all_to_all(half, ("x", "y"), split_axis=0, concat_axis=0, tiled=True)
    mixed = (hidden + jnp.sum(parts.astype(f32), axis=0)).astype(bf16)
    back = lax.all_to_all(
        mixed.reshape(n_z, SLOTS, width), "z", split_axis=0, concat_axis=0, tiled=True
    )
    back = back.reshape(slots, width)
    out = jnp.einsum("sr,sc->rc", table.astype(bf16), back, preferred_element_type=f32)
    return out.astype(bf16)


def solution(mesh):
    n_x = GROUP
    n_z = mesh.shape["dp"] // n_x
    n_y = mesh.shape["cuts"] // CORES
    fine = Mesh(mesh.devices.reshape(n_z, n_x, n_y, CORES), ("z", "x", "y", "core"))
    rows, cols = ("z", "x"), ("y", "core")
    placed = (
        P(rows, cols),
        P(rows, cols),
        P(rows, cols),
        P(rows, None, cols),
        P(rows, None, cols),
        P(rows),
        P(rows, None),
        P(),
        P(cols, None),
        P(rows, None),
        P(rows, None, cols),
        P(rows, cols, None),
    )
    return jax.shard_map(
        on_device, mesh=fine, in_specs=placed, out_specs=P(rows, cols), check_vma=False
    )
```

```python
import functools

import jax
import jax.numpy as jnp
from jax import lax
from jax.experimental import pallas as pl
from jax.experimental.pallas import tpu as pltpu
from jax.sharding import Mesh
from jax.sharding import PartitionSpec as P

HD = 128
GROUP = 4
CORES = 2
SLOTS = 2


def attend_kernel(
    n_y,
    queries,
    new_keys,
    new_values,
    key_cache,
    value_cache,
    lengths,
    resid,
    w_out,
    keep,
    give,
    weights,
    sem,
):
    f32, bf16 = jnp.float32, jnp.bfloat16
    core, my_y = lax.axis_index("core"), lax.axis_index("y")
    copy = pltpu.make_async_copy(w_out, weights, sem)
    copy.start()
    count, feats = queries.shape
    spots = key_cache.shape[0]
    length = spots // count
    scale = 1.0 / HD**0.5
    row = lax.broadcasted_iota(jnp.int32, (count, spots), 0)
    spot = lax.broadcasted_iota(jnp.int32, (count, spots), 1)
    limit = jnp.zeros((count, spots), jnp.int32)
    for r in range(count):
        limit = jnp.where(row == r, r * length + lengths[r], limit)
    valid = (spot >= row * length) & (spot < limit)
    heads = []
    for h in range(feats // HD):
        cols = slice(h * HD, (h + 1) * HD)
        query = queries[:, cols]
        scores = lax.dot_general(
            query, key_cache[:, cols], (((1,), (1,)), ((), ())), preferred_element_type=f32
        )
        scores = jnp.where(valid, scores * scale, -1e30)
        fresh = query.astype(f32) * new_keys[:, cols].astype(f32)
        fresh = jnp.sum(fresh, axis=-1, keepdims=True) * scale
        peak = jnp.maximum(jnp.max(scores, axis=-1, keepdims=True), fresh)
        pcache = jnp.where(valid, jnp.exp(scores - peak), 0.0)
        pnew = jnp.exp(fresh - peak)
        total = jnp.sum(pcache, axis=-1, keepdims=True) + pnew
        pcache = (pcache / total).astype(bf16)
        pnew = (pnew / total).astype(bf16).astype(f32)
        summed = jnp.dot(pcache, value_cache[:, cols], preferred_element_type=f32)
        summed = summed + pnew * new_values[:, cols].astype(f32)
        heads.append(summed.astype(bf16))
    heads_out = jnp.concatenate(heads, axis=1)
    copy.wait()
    width = weights.shape[1] // (n_y * CORES)
    for y in range(n_y):
        pair = []
        for c in range(CORES):
            cols = pl.ds((y * CORES + c) * width, width)
            pair.append(jnp.dot(heads_out, weights[:, cols], preferred_element_type=f32))
        low = resid[:, pl.ds(y * CORES * width, width)].astype(f32)
        high = resid[:, pl.ds((y * CORES + 1) * width, width)].astype(f32)
        rest = jnp.where(my_y == y, jnp.where(core == 0, low, high), 0.0)
        keep[:, pl.ds(y * width, width)] = jnp.where(core == 0, pair[0], pair[1]) + rest
        give[:, pl.ds(y * width, width)] = jnp.where(core == 0, pair[1], pair[0])


def attend(
    n_y, queries, new_keys, new_values, key_cache, value_cache, lengths, resid, w_out
):
    count, feats = queries.shape
    spots = count * key_cache.shape[1]
    vmem, smem = pl.BlockSpec(memory_space=pltpu.VMEM), pl.BlockSpec(memory_space=pltpu.SMEM)
    half = jax.ShapeDtypeStruct((count, w_out.shape[1] // CORES), jnp.float32)
    return pl.pallas_call(
        functools.partial(attend_kernel, n_y),
        out_shape=(half, half),
        in_specs=[vmem] * 5 + [smem, vmem, pl.BlockSpec(memory_space=pl.ANY)],
        out_specs=(vmem, vmem),
        scratch_shapes=[pltpu.VMEM(w_out.shape, w_out.dtype), pltpu.SemaphoreType.DMA],
        name="attend",
    )(
        queries,
        new_keys,
        new_values,
        key_cache.reshape(spots, feats),
        value_cache.reshape(spots, feats),
        lengths,
        resid,
        w_out,
    )


def expert_kernel(n_x, n_y, pair, gain, w_up, w_down, keep, give, up, down, sems):
    f32, bf16 = jnp.float32, jnp.bfloat16
    core = lax.axis_index("core")
    copies = [
        pltpu.make_async_copy(w_up, up, sems.at[0]),
        pltpu.make_async_copy(w_down, down, sems.at[1]),
    ]
    for copy in copies:
        copy.start()
    slots, width = pair.shape[2:]
    width_all = n_y * CORES * width
    blocks = []
    squares = jnp.zeros((n_x * slots, 1), f32)
    for y in range(n_y):
        for c in range(CORES):
            block = [pair[c, x * n_y + y].astype(f32) for x in range(n_x)]
            block = jnp.concatenate(block, axis=0)
            squares = squares + jnp.sum(block * block, axis=-1, keepdims=True)
            blocks.append(block)
    inverse = lax.rsqrt(squares * (1.0 / width_all) + 1e-06)
    normed = [
        (block * inverse * gain[:, pl.ds(i * width, width)]).astype(bf16)
        for i, block in enumerate(blocks)
    ]
    copies[0].wait()
    units = jnp.zeros((n_x * slots, up.shape[1]), f32)
    for i, block in enumerate(normed):
        units = units + jnp.dot(block, up[pl.ds(i * width, width), :], preferred_element_type=f32)
    act = jax.nn.gelu(units).astype(bf16)
    copies[1].wait()
    for y in range(n_y):
        both = []
        for c in range(CORES):
            cols = pl.ds((y * CORES + c) * width, width)
            both.append(jnp.dot(act, down[:, cols], preferred_element_type=f32))
        own = jnp.where(core == 0, both[0], both[1])
        other = jnp.where(core == 0, both[1], both[0]).astype(bf16)
        for x in range(n_x):
            keep[x * n_y + y] = own[x * slots : (x + 1) * slots]
            give[x * n_y + y] = other[x * slots : (x + 1) * slots]


def run_expert(n_x, n_y, pair, norm_gain, w_up, w_down):
    vmem, anywhere = pl.BlockSpec(memory_space=pltpu.VMEM), pl.BlockSpec(memory_space=pl.ANY)
    return pl.pallas_call(
        functools.partial(expert_kernel, n_x, n_y),
        out_shape=(
            jax.ShapeDtypeStruct(pair.shape[1:], jnp.float32),
            jax.ShapeDtypeStruct(pair.shape[1:], jnp.bfloat16),
        ),
        in_specs=[vmem, vmem, anywhere, anywhere],
        out_specs=(vmem, vmem),
        scratch_shapes=[
            pltpu.VMEM(w_up.shape, w_up.dtype),
            pltpu.VMEM(w_down.shape, w_down.dtype),
            pltpu.SemaphoreType.DMA((2,)),
        ],
        name="expert",
    )(pair, norm_gain[None, :], w_up, w_down)


def on_device(
    queries,
    new_keys,
    new_values,
    key_cache,
    value_cache,
    lengths,
    resid,
    norm_gain,
    w_out,
    experts,
    w_up,
    w_down,
):
    bf16, f32 = jnp.bfloat16, jnp.float32
    count, width_all = resid.shape
    n_z, n_x, n_y = lax.axis_size("z"), lax.axis_size("x"), lax.axis_size("y")
    width = width_all // (n_y * CORES)
    core = lax.axis_index("core")
    my_y = lax.axis_index("y")

    keep, give = attend(
        n_y, queries, new_keys, new_values, key_cache, value_cache, lengths, resid, w_out
    )
    given = lax.all_gather(give, "core", axis=0)

    ids = experts[:, 0]
    order_idx = jnp.arange(count, dtype=jnp.int32)
    earlier = (ids[:, None] == ids[None, :]) & (order_idx[:, None] > order_idx[None, :])
    slot_id = ids * SLOTS + jnp.sum(earlier.astype(jnp.int32), axis=1)
    table = jnp.arange(n_z * SLOTS, dtype=jnp.int32)[:, None] == slot_id[None, :]

    chip = keep + lax.dynamic_index_in_dim(given, 1 - core, 0, keepdims=False)
    chip = chip.astype(bf16).reshape(count, n_y, width)
    packed = jnp.einsum("sr,ryc->syc", table.astype(bf16), chip, preferred_element_type=f32)
    packed = packed.astype(bf16).reshape(n_z, SLOTS, n_y, width).transpose(0, 2, 1, 3)
    packed = packed.reshape(n_z * n_y, SLOTS, width)
    got = lax.all_to_all(packed, ("z", "y"), split_axis=0, concat_axis=0, tiled=True)
    slots = n_z * SLOTS
    hidden = jnp.sum(got.reshape(n_z, n_y, SLOTS, width).astype(f32), axis=1).reshape(slots, width)

    spread = jnp.broadcast_to(hidden.astype(bf16)[None], (n_x * n_y, slots, width))
    plane = lax.all_to_all(spread, ("x", "y"), split_axis=0, concat_axis=0, tiled=True)
    pair = lax.all_gather(plane, "core", axis=0)
    keep, give = run_expert(n_x, n_y, pair, norm_gain, w_up[0], w_down[0])
    given = lax.all_gather(give, "core", axis=0)
    half = keep + lax.dynamic_index_in_dim(given, 1 - core, 0, keepdims=False).astype(f32)
    half = half.astype(bf16)
    parts = lax.all_to_all(half, ("x", "y"), split_axis=0, concat_axis=0, tiled=True)
    mixed = (hidden + jnp.sum(parts.astype(f32), axis=0)).astype(bf16)
    back = lax.all_to_all(
        mixed.reshape(n_z, SLOTS, width), "z", split_axis=0, concat_axis=0, tiled=True
    )
    back = back.reshape(slots, width)
    out = jnp.einsum("sr,sc->rc", table.astype(bf16), back, preferred_element_type=f32)
    return out.astype(bf16)


def solution(mesh):
    n_x = GROUP
    n_z = mesh.shape["dp"] // n_x
    n_y = mesh.shape["cuts"] // CORES
    fine = Mesh(mesh.devices.reshape(n_z, n_x, n_y, CORES), ("z", "x", "y", "core"))
    rows, cols = ("z", "x"), ("y", "core")
    placed = (
        P(rows, cols),
        P(rows, cols),
        P(rows, cols),
        P(rows, None, cols),
        P(rows, None, cols),
        P(rows),
        P(rows, None),
        P(),
        P(cols, None),
        P(rows, None),
        P(rows, None, cols),
        P(rows, cols, None),
    )
    return jax.shard_map(
        on_device, mesh=fine, in_specs=placed, out_specs=P(rows, cols), check_vma=False
    )
```

```python
import functools

import jax
import jax.numpy as jnp
from jax import lax
from jax.experimental import pallas as pl
from jax.experimental.pallas import tpu as pltpu
from jax.sharding import Mesh
from jax.sharding import PartitionSpec as P

HD = 128
GROUP = 4
CORES = 2
SLOTS = 2


def in_vmem(shape, dtype):
    return pltpu.VMEM(shape, dtype)


def attend_kernel(n_y, *refs):
    f32, bf16 = jnp.float32, jnp.bfloat16
    sources, (keep, give, table), held, sems = refs[:9], refs[9:12], refs[12:21], refs[21]
    core, my_y = lax.axis_index("core"), lax.axis_index("y")
    copies = [
        pltpu.make_async_copy(source, target, sems.at[i])
        for i, (source, target) in enumerate(zip(sources, held))
    ]
    for copy in copies:
        copy.start()
    lengths, ids, queries, key_cache, new_keys, value_cache, new_values, w_out, resid = held
    count, feats = queries.shape
    spots = key_cache.shape[0]
    length = spots // count
    scale = 1.0 / HD**0.5
    for copy in copies[:2]:
        copy.wait()
    row = lax.broadcasted_iota(jnp.int32, (count, spots), 0)
    spot = lax.broadcasted_iota(jnp.int32, (count, spots), 1)
    limit = jnp.zeros((count, spots), jnp.int32)
    for r in range(count):
        limit = jnp.where(row == r, r * length + lengths[r], limit)
    valid = (spot >= row * length) & (spot < limit)
    slot = lax.broadcasted_iota(jnp.int32, table.shape, 0)
    name = lax.broadcasted_iota(jnp.int32, table.shape, 1)
    hot = jnp.zeros(table.shape, f32)
    for r in range(count):
        place = ids[r] * SLOTS
        for q in range(r):
            place = place + (ids[q] == ids[r]).astype(jnp.int32)
        hot = jnp.where((name == r) & (slot == place), 1.0, hot)
    table[...] = hot.astype(bf16)
    for copy in copies[2:5]:
        copy.wait()
    probs = []
    for h in range(feats // HD):
        cols = slice(h * HD, (h + 1) * HD)
        query = queries[:, cols]
        scores = lax.dot_general(
            query, key_cache[:, cols], (((1,), (1,)), ((), ())), preferred_element_type=f32
        )
        scores = jnp.where(valid, scores * scale, -1e30)
        fresh = query.astype(f32) * new_keys[:, cols].astype(f32)
        fresh = jnp.sum(fresh, axis=-1, keepdims=True) * scale
        peak = jnp.maximum(jnp.max(scores, axis=-1, keepdims=True), fresh)
        pcache = jnp.where(valid, jnp.exp(scores - peak), 0.0)
        pnew = jnp.exp(fresh - peak)
        total = jnp.sum(pcache, axis=-1, keepdims=True) + pnew
        probs.append(((pcache / total).astype(bf16), (pnew / total).astype(bf16).astype(f32)))
    for copy in copies[5:7]:
        copy.wait()
    heads = []
    for h, (pcache, pnew) in enumerate(probs):
        cols = slice(h * HD, (h + 1) * HD)
        summed = jnp.dot(pcache, value_cache[:, cols], preferred_element_type=f32)
        summed = summed + pnew * new_values[:, cols].astype(f32)
        heads.append(summed.astype(bf16))
    heads_out = jnp.concatenate(heads, axis=1)
    for copy in copies[7:]:
        copy.wait()
    width = w_out.shape[1] // (n_y * CORES)
    for y in range(n_y):
        pair = []
        for c in range(CORES):
            cols = pl.ds((y * CORES + c) * width, width)
            pair.append(jnp.dot(heads_out, w_out[:, cols], preferred_element_type=f32))
        low = resid[:, pl.ds(y * CORES * width, width)].astype(f32)
        high = resid[:, pl.ds((y * CORES + 1) * width, width)].astype(f32)
        rest = jnp.where(my_y == y, jnp.where(core == 0, low, high), 0.0)
        keep[:, pl.ds(y * width, width)] = jnp.where(core == 0, pair[0], pair[1]) + rest
        give[:, pl.ds(y * width, width)] = jnp.where(core == 0, pair[1], pair[0])


def attend(
    n_y,
    slots,
    queries,
    new_keys,
    new_values,
    key_cache,
    value_cache,
    lengths,
    resid,
    w_out,
    ids,
):
    count, feats = queries.shape
    spots = count * key_cache.shape[1]
    args = (
        lengths,
        ids,
        queries,
        key_cache.reshape(spots, feats),
        new_keys,
        value_cache.reshape(spots, feats),
        new_values,
        w_out,
        resid,
    )
    half = in_vmem((count, w_out.shape[1] // CORES), jnp.float32)
    vmem, anywhere = pl.BlockSpec(memory_space=pltpu.VMEM), pl.BlockSpec(memory_space=pl.ANY)
    spaces = [pltpu.SMEM] * 2 + [pltpu.VMEM] * 7
    return pl.pallas_call(
        functools.partial(attend_kernel, n_y),
        out_shape=(half, half, in_vmem((slots, count), jnp.bfloat16)),
        in_specs=[anywhere] * len(args),
        out_specs=(vmem,) * 3,
        scratch_shapes=[space(arg.shape, arg.dtype) for space, arg in zip(spaces, args)]
        + [pltpu.SemaphoreType.DMA((len(args),))],
        name="attend",
    )(*args)


def expert_kernel(n_x, n_y, pair, gain, up, down, keep, give, normed):
    f32, bf16 = jnp.float32, jnp.bfloat16
    core = lax.axis_index("core")
    slots, width = pair.shape[2:]
    width_all = n_y * CORES * width
    blocks = [(y, c) for y in range(n_y) for c in range(CORES)]
    for x in range(n_x):
        squares = jnp.zeros((slots, width), f32)
        for y, c in blocks:
            block = pair[c, x * n_y + y].astype(f32)
            squares = squares + block * block
        meansq = jnp.sum(squares, axis=-1, keepdims=True) * (1.0 / width_all)
        inverse = lax.rsqrt(meansq + 1e-06)
        for y, c in blocks:
            cols = pl.ds((y * CORES + c) * width, width)
            block = pair[c, x * n_y + y].astype(f32) * inverse * gain[:, cols]
            normed[pl.ds(x * slots, slots), cols] = block.astype(bf16)
    units = jnp.dot(normed[...], up[...], preferred_element_type=f32)
    act = jax.nn.gelu(units).astype(bf16)
    for y in range(n_y):
        both = []
        for c in range(CORES):
            cols = pl.ds((y * CORES + c) * width, width)
            both.append(jnp.dot(act, down[:, cols], preferred_element_type=f32))
        own = jnp.where(core == 0, both[0], both[1])
        other = jnp.where(core == 0, both[1], both[0]).astype(bf16)
        for x in range(n_x):
            keep[x * n_y + y] = own[x * slots : (x + 1) * slots]
            give[x * n_y + y] = other[x * slots : (x + 1) * slots]


def run_expert(n_x, n_y, pair, norm_gain, w_up, w_down):
    vmem = pl.BlockSpec(memory_space=pltpu.VMEM)
    args = [
        pltpu.with_memory_space_constraint(arg, pltpu.VMEM)
        for arg in (pair, norm_gain[None, :], w_up, w_down)
    ]
    return pl.pallas_call(
        functools.partial(expert_kernel, n_x, n_y),
        out_shape=(
            in_vmem(pair.shape[1:], jnp.float32),
            in_vmem(pair.shape[1:], jnp.bfloat16),
        ),
        in_specs=[vmem] * 4,
        out_specs=(vmem, vmem),
        scratch_shapes=[pltpu.VMEM((n_x * pair.shape[2], w_up.shape[0]), jnp.bfloat16)],
        name="expert",
    )(*args)


def on_device(
    queries,
    new_keys,
    new_values,
    key_cache,
    value_cache,
    lengths,
    resid,
    norm_gain,
    w_out,
    experts,
    w_up,
    w_down,
):
    bf16, f32 = jnp.bfloat16, jnp.float32
    count, width_all = resid.shape
    n_z, n_x, n_y = lax.axis_size("z"), lax.axis_size("x"), lax.axis_size("y")
    width = width_all // (n_y * CORES)
    core = lax.axis_index("core")

    slots = n_z * SLOTS
    keep, give, table = attend(
        n_y,
        slots,
        queries,
        new_keys,
        new_values,
        key_cache,
        value_cache,
        lengths,
        resid,
        w_out,
        experts[:, 0],
    )
    given = lax.all_gather(give, "core", axis=0)
    chip = keep + lax.dynamic_index_in_dim(given, 1 - core, 0, keepdims=False)
    chip = chip.astype(bf16).reshape(count, n_y, width)
    packed = jnp.einsum("sr,ryc->syc", table, chip, preferred_element_type=f32)
    packed = packed.astype(bf16).reshape(n_z, SLOTS, n_y, width).transpose(0, 2, 1, 3)
    packed = packed.reshape(n_z * n_y, SLOTS, width)
    got = lax.all_to_all(packed, ("z", "y"), split_axis=0, concat_axis=0, tiled=True)
    hidden = jnp.sum(got.reshape(n_z, n_y, SLOTS, width).astype(f32), axis=1).reshape(slots, width)

    spread = jnp.broadcast_to(hidden.astype(bf16)[None], (n_x * n_y, slots, width))
    plane = lax.all_to_all(spread, ("x", "y"), split_axis=0, concat_axis=0, tiled=True)
    pair = lax.all_gather(plane, "core", axis=0)
    keep, give = run_expert(n_x, n_y, pair, norm_gain, w_up[0], w_down[0])
    given = lax.all_gather(give, "core", axis=0)
    half = keep + lax.dynamic_index_in_dim(given, 1 - core, 0, keepdims=False).astype(f32)
    half = half.astype(bf16)
    parts = lax.all_to_all(half, ("x", "y"), split_axis=0, concat_axis=0, tiled=True)
    mixed = (hidden + jnp.sum(parts.astype(f32), axis=0)).astype(bf16)
    back = lax.all_to_all(
        mixed.reshape(n_z, SLOTS, width), "z", split_axis=0, concat_axis=0, tiled=True
    )
    back = back.reshape(slots, width)
    out = jnp.einsum("sr,sc->rc", table, back, preferred_element_type=f32)
    return out.astype(bf16)


def solution(mesh):
    n_x = GROUP
    n_z = mesh.shape["dp"] // n_x
    n_y = mesh.shape["cuts"] // CORES
    fine = Mesh(mesh.devices.reshape(n_z, n_x, n_y, CORES), ("z", "x", "y", "core"))
    rows, cols = ("z", "x"), ("y", "core")
    placed = (
        P(rows, cols),
        P(rows, cols),
        P(rows, cols),
        P(rows, None, cols),
        P(rows, None, cols),
        P(rows),
        P(rows, None),
        P(),
        P(cols, None),
        P(rows, None),
        P(rows, None, cols),
        P(rows, cols, None),
    )
    return jax.shard_map(
        on_device, mesh=fine, in_specs=placed, out_specs=P(rows, cols), check_vma=False
    )
```

```python
import functools

import jax
import jax.numpy as jnp
from jax import lax
from jax.experimental import pallas as pl
from jax.experimental.pallas import tpu as pltpu
from jax.sharding import Mesh
from jax.sharding import PartitionSpec as P

HD = 128
GROUP = 4
CORES = 2
SLOTS = 2


def in_vmem(shape, dtype):
    return pltpu.VMEM(shape, dtype)


def attend_kernel(n_y, *refs):
    f32, bf16 = jnp.float32, jnp.bfloat16
    sources, (keep, give, table), held, sems = refs[:9], refs[9:12], refs[12:21], refs[21]
    core, my_y = lax.axis_index("core"), lax.axis_index("y")
    copies = [
        pltpu.make_async_copy(source, target, sems.at[i])
        for i, (source, target) in enumerate(zip(sources, held))
    ]
    for copy in copies:
        copy.start()
    lengths, ids, queries, key_cache, new_keys, value_cache, new_values, w_out, resid = held
    count, feats = queries.shape
    spots = key_cache.shape[0]
    length = spots // count
    scale = 1.0 / HD**0.5
    for copy in copies[:2]:
        copy.wait()
    row = lax.broadcasted_iota(jnp.int32, (count, spots), 0)
    spot = lax.broadcasted_iota(jnp.int32, (count, spots), 1)
    limit = jnp.zeros((count, spots), jnp.int32)
    for r in range(count):
        limit = jnp.where(row == r, r * length + lengths[r], limit)
    valid = (spot >= row * length) & (spot < limit)
    slot = lax.broadcasted_iota(jnp.int32, table.shape, 0)
    name = lax.broadcasted_iota(jnp.int32, table.shape, 1)
    hot = jnp.zeros(table.shape, f32)
    for r in range(count):
        place = ids[r] * SLOTS
        for q in range(r):
            place = place + (ids[q] == ids[r]).astype(jnp.int32)
        hot = jnp.where((name == r) & (slot == place), 1.0, hot)
    table[...] = hot.astype(bf16)
    for copy in copies[2:5]:
        copy.wait()
    probs = []
    for h in range(feats // HD):
        cols = slice(h * HD, (h + 1) * HD)
        query = queries[:, cols]
        scores = lax.dot_general(
            query, key_cache[:, cols], (((1,), (1,)), ((), ())), preferred_element_type=f32
        )
        scores = jnp.where(valid, scores * scale, -1e30)
        fresh = query.astype(f32) * new_keys[:, cols].astype(f32)
        fresh = jnp.sum(fresh, axis=-1, keepdims=True) * scale
        peak = jnp.maximum(jnp.max(scores, axis=-1, keepdims=True), fresh)
        pcache = jnp.where(valid, jnp.exp(scores - peak), 0.0)
        pnew = jnp.exp(fresh - peak)
        total = jnp.sum(pcache, axis=-1, keepdims=True) + pnew
        probs.append(((pcache / total).astype(bf16), (pnew / total).astype(bf16).astype(f32)))
    for copy in copies[5:7]:
        copy.wait()
    heads = []
    for h, (pcache, pnew) in enumerate(probs):
        cols = slice(h * HD, (h + 1) * HD)
        summed = jnp.dot(pcache, value_cache[:, cols], preferred_element_type=f32)
        summed = summed + pnew * new_values[:, cols].astype(f32)
        heads.append(summed.astype(bf16))
    heads_out = jnp.concatenate(heads, axis=1)
    for copy in copies[7:]:
        copy.wait()
    width = w_out.shape[1] // (n_y * CORES)
    for y in range(n_y):
        pair = []
        for c in range(CORES):
            cols = pl.ds((y * CORES + c) * width, width)
            pair.append(jnp.dot(heads_out, w_out[:, cols], preferred_element_type=f32))
        low = resid[:, pl.ds(y * CORES * width, width)].astype(f32)
        high = resid[:, pl.ds((y * CORES + 1) * width, width)].astype(f32)
        rest = jnp.where(my_y == y, jnp.where(core == 0, low, high), 0.0)
        keep[:, pl.ds(y * width, width)] = jnp.where(core == 0, pair[0], pair[1]) + rest
        give[:, pl.ds(y * width, width)] = jnp.where(core == 0, pair[1], pair[0])


def attend(
    n_y,
    slots,
    queries,
    new_keys,
    new_values,
    key_cache,
    value_cache,
    lengths,
    resid,
    w_out,
    ids,
):
    count, feats = queries.shape
    spots = count * key_cache.shape[1]
    args = (
        lengths,
        ids,
        queries,
        key_cache.reshape(spots, feats),
        new_keys,
        value_cache.reshape(spots, feats),
        new_values,
        w_out,
        resid,
    )
    half = in_vmem((count, w_out.shape[1] // CORES), jnp.float32)
    vmem, anywhere = pl.BlockSpec(memory_space=pltpu.VMEM), pl.BlockSpec(memory_space=pl.ANY)
    spaces = [pltpu.SMEM] * 2 + [pltpu.VMEM] * 7
    return pl.pallas_call(
        functools.partial(attend_kernel, n_y),
        out_shape=(half, half, in_vmem((slots, count), jnp.bfloat16)),
        in_specs=[anywhere] * len(args),
        out_specs=(vmem,) * 3,
        scratch_shapes=[space(arg.shape, arg.dtype) for space, arg in zip(spaces, args)]
        + [pltpu.SemaphoreType.DMA((len(args),))],
        name="attend",
    )(*args)


def expert_kernel(n_x, n_y, pair, gain, up, down, pieces, normed):
    f32, bf16 = jnp.float32, jnp.bfloat16
    slots, width = pair.shape[2:]
    width_all = n_y * CORES * width
    blocks = [(y, c) for y in range(n_y) for c in range(CORES)]
    for x in range(n_x):
        squares = jnp.zeros((slots, width), f32)
        for y, c in blocks:
            block = pair[c, x * n_y + y].astype(f32)
            squares = squares + block * block
        meansq = jnp.sum(squares, axis=-1, keepdims=True) * (1.0 / width_all)
        inverse = lax.rsqrt(meansq + 1e-06)
        for y, c in blocks:
            cols = pl.ds((y * CORES + c) * width, width)
            block = pair[c, x * n_y + y].astype(f32) * inverse * gain[:, cols]
            normed[pl.ds(x * slots, slots), cols] = block.astype(bf16)
    units = jnp.dot(normed[...], up[...], preferred_element_type=f32)
    act = jax.nn.gelu(units).astype(bf16)
    for y in range(n_y):
        cols = pl.ds(y * CORES * width, CORES * width)
        piece = jnp.dot(act, down[:, cols], preferred_element_type=f32).astype(bf16)
        for x in range(n_x):
            pieces[x * n_y + y] = piece[x * slots : (x + 1) * slots]


def run_expert(n_x, n_y, pair, norm_gain, w_up, w_down):
    vmem = pl.BlockSpec(memory_space=pltpu.VMEM)
    args = [
        pltpu.with_memory_space_constraint(arg, pltpu.VMEM)
        for arg in (pair, norm_gain[None, :], w_up, w_down)
    ]
    return pl.pallas_call(
        functools.partial(expert_kernel, n_x, n_y),
        out_shape=in_vmem(pair.shape[1:3] + (CORES * pair.shape[3],), jnp.bfloat16),
        in_specs=[vmem] * 4,
        out_specs=vmem,
        scratch_shapes=[pltpu.VMEM((n_x * pair.shape[2], w_up.shape[0]), jnp.bfloat16)],
        name="expert",
    )(*args)


def on_device(
    queries,
    new_keys,
    new_values,
    key_cache,
    value_cache,
    lengths,
    resid,
    norm_gain,
    w_out,
    experts,
    w_up,
    w_down,
):
    bf16, f32 = jnp.bfloat16, jnp.float32
    count, width_all = resid.shape
    n_z, n_x, n_y = lax.axis_size("z"), lax.axis_size("x"), lax.axis_size("y")
    width = width_all // (n_y * CORES)
    core = lax.axis_index("core")

    slots = n_z * SLOTS
    keep, give, table = attend(
        n_y,
        slots,
        queries,
        new_keys,
        new_values,
        key_cache,
        value_cache,
        lengths,
        resid,
        w_out,
        experts[:, 0],
    )
    given = lax.all_gather(give, "core", axis=0)
    chip = keep + lax.dynamic_index_in_dim(given, 1 - core, 0, keepdims=False)
    chip = chip.astype(bf16).reshape(count, n_y, width)
    packed = jnp.einsum("sr,ryc->syc", table, chip, preferred_element_type=f32)
    packed = packed.astype(bf16).reshape(n_z, SLOTS, n_y, width).transpose(0, 2, 1, 3)
    packed = packed.reshape(n_z * n_y, SLOTS, width)
    got = lax.all_to_all(packed, ("z", "y"), split_axis=0, concat_axis=0, tiled=True)
    hidden = jnp.sum(got.reshape(n_z, n_y, SLOTS, width).astype(f32), axis=1).reshape(slots, width)

    spread = jnp.broadcast_to(hidden.astype(bf16)[None], (n_x * n_y, slots, width))
    plane = lax.all_to_all(spread, ("x", "y"), split_axis=0, concat_axis=0, tiled=True)
    pair = lax.all_gather(plane, "core", axis=0)
    pieces = run_expert(n_x, n_y, pair, norm_gain, w_up[0], w_down[0])
    parts = lax.all_to_all(pieces, ("x", "y"), split_axis=0, concat_axis=0, tiled=True)
    both = jnp.sum(parts.astype(f32), axis=0).reshape(n_z, SLOTS, CORES, width)
    mine = (jnp.arange(CORES) == core)[None, None, :, None]
    both = both + jnp.where(mine, hidden.reshape(n_z, SLOTS, 1, width), 0.0)
    both = both.astype(bf16).transpose(0, 2, 1, 3).reshape(n_z * CORES, SLOTS, width)
    back = lax.all_to_all(both, ("z", "core"), split_axis=0, concat_axis=0, tiled=True)
    back = back.reshape(n_z, CORES, SLOTS, width)
    spots = table.reshape(n_z, SLOTS, count)
    out = jnp.einsum("zsr,zksc->rc", spots, back, preferred_element_type=f32)
    return out.astype(bf16)


def solution(mesh):
    n_x = GROUP
    n_z = mesh.shape["dp"] // n_x
    n_y = mesh.shape["cuts"] // CORES
    fine = Mesh(mesh.devices.reshape(n_z, n_x, n_y, CORES), ("z", "x", "y", "core"))
    rows, cols = ("z", "x"), ("y", "core")
    placed = (
        P(rows, cols),
        P(rows, cols),
        P(rows, cols),
        P(rows, None, cols),
        P(rows, None, cols),
        P(rows),
        P(rows, None),
        P(),
        P(cols, None),
        P(rows, None),
        P(rows, None, cols),
        P(rows, cols, None),
    )
    return jax.shard_map(
        on_device, mesh=fine, in_specs=placed, out_specs=P(rows, cols), check_vma=False
    )
```

```python
import functools

import jax
import jax.numpy as jnp
from jax import lax
from jax.experimental import pallas as pl
from jax.experimental.pallas import tpu as pltpu
from jax.sharding import Mesh
from jax.sharding import PartitionSpec as P

HD = 128
GROUP = 4
CORES = 2
SLOTS = 2


def in_vmem(shape, dtype):
    return pltpu.VMEM(shape, dtype)


def attend_kernel(n_y, *refs):
    f32, bf16 = jnp.float32, jnp.bfloat16
    sources, (keep, give, table), held, sems = refs[:9], refs[9:12], refs[12:21], refs[21]
    core, my_y = lax.axis_index("core"), lax.axis_index("y")
    copies = [
        pltpu.make_async_copy(source, target, sems.at[i])
        for i, (source, target) in enumerate(zip(sources, held))
    ]
    for copy in copies:
        copy.start()
    lengths, ids, queries, key_cache, new_keys, value_cache, new_values, w_out, resid = held
    count, feats = queries.shape
    spots = key_cache.shape[0]
    length = spots // count
    scale = 1.0 / HD**0.5
    for copy in copies[:2]:
        copy.wait()
    row = lax.broadcasted_iota(jnp.int32, (count, spots), 0)
    spot = lax.broadcasted_iota(jnp.int32, (count, spots), 1)
    limit = jnp.zeros((count, spots), jnp.int32)
    for r in range(count):
        limit = jnp.where(row == r, r * length + lengths[r], limit)
    valid = (spot >= row * length) & (spot < limit)
    slot = lax.broadcasted_iota(jnp.int32, table.shape, 0)
    name = lax.broadcasted_iota(jnp.int32, table.shape, 1)
    hot = jnp.zeros(table.shape, f32)
    for r in range(count):
        place = ids[r] * SLOTS
        for q in range(r):
            place = place + (ids[q] == ids[r]).astype(jnp.int32)
        hot = jnp.where((name == r) & (slot == place), 1.0, hot)
    table[...] = hot.astype(bf16)
    for copy in copies[2:5]:
        copy.wait()
    probs = []
    for h in range(feats // HD):
        cols = slice(h * HD, (h + 1) * HD)
        query = queries[:, cols]
        scores = lax.dot_general(
            query, key_cache[:, cols], (((1,), (1,)), ((), ())), preferred_element_type=f32
        )
        scores = jnp.where(valid, scores * scale, -1e30)
        fresh = query.astype(f32) * new_keys[:, cols].astype(f32)
        fresh = jnp.sum(fresh, axis=-1, keepdims=True) * scale
        peak = jnp.maximum(jnp.max(scores, axis=-1, keepdims=True), fresh)
        pcache = jnp.where(valid, jnp.exp(scores - peak), 0.0)
        pnew = jnp.exp(fresh - peak)
        total = jnp.sum(pcache, axis=-1, keepdims=True) + pnew
        probs.append(((pcache / total).astype(bf16), (pnew / total).astype(bf16).astype(f32)))
    for copy in copies[5:7]:
        copy.wait()
    heads = []
    for h, (pcache, pnew) in enumerate(probs):
        cols = slice(h * HD, (h + 1) * HD)
        summed = jnp.dot(pcache, value_cache[:, cols], preferred_element_type=f32)
        summed = summed + pnew * new_values[:, cols].astype(f32)
        heads.append(summed.astype(bf16))
    heads_out = jnp.concatenate(heads, axis=1)
    for copy in copies[7:]:
        copy.wait()
    width = w_out.shape[1] // (n_y * CORES)
    for y in range(n_y):
        pair = []
        for c in range(CORES):
            cols = pl.ds((y * CORES + c) * width, width)
            pair.append(jnp.dot(heads_out, w_out[:, cols], preferred_element_type=f32))
        low = resid[:, pl.ds(y * CORES * width, width)].astype(f32)
        high = resid[:, pl.ds((y * CORES + 1) * width, width)].astype(f32)
        rest = jnp.where(my_y == y, jnp.where(core == 0, low, high), 0.0)
        keep[:, pl.ds(y * width, width)] = jnp.where(core == 0, pair[0], pair[1]) + rest
        give[:, pl.ds(y * width, width)] = jnp.where(core == 0, pair[1], pair[0])


def attend(
    n_y,
    slots,
    queries,
    new_keys,
    new_values,
    key_cache,
    value_cache,
    lengths,
    resid,
    w_out,
    ids,
):
    count, feats = queries.shape
    spots = count * key_cache.shape[1]
    args = (
        lengths,
        ids,
        queries,
        key_cache.reshape(spots, feats),
        new_keys,
        value_cache.reshape(spots, feats),
        new_values,
        w_out,
        resid,
    )
    half = in_vmem((count, w_out.shape[1] // CORES), jnp.float32)
    vmem, anywhere = pl.BlockSpec(memory_space=pltpu.VMEM), pl.BlockSpec(memory_space=pl.ANY)
    spaces = [pltpu.SMEM] * 2 + [pltpu.VMEM] * 7
    return pl.pallas_call(
        functools.partial(attend_kernel, n_y),
        out_shape=(half, half, in_vmem((slots, count), jnp.bfloat16)),
        in_specs=[anywhere] * len(args),
        out_specs=(vmem,) * 3,
        scratch_shapes=[space(arg.shape, arg.dtype) for space, arg in zip(spaces, args)]
        + [pltpu.SemaphoreType.DMA((len(args),))],
        name="attend",
    )(*args)


def units_kernel(n_x, n_y, plane, gain, up, up_other, partial):
    f32, bf16 = jnp.float32, jnp.bfloat16
    core = lax.axis_index("core")
    slots, width = plane.shape[1:]
    units = up.shape[1]
    rows = n_x * slots
    own = jnp.zeros((rows, units), f32)
    other = jnp.zeros((rows, units), f32)
    squares = jnp.zeros((rows, width), f32)
    for y in range(n_y):
        block = [plane[x * n_y + y].astype(f32) for x in range(n_x)]
        block = jnp.concatenate(block, axis=0)
        squares = squares + block * block
        low = gain[:, pl.ds(y * CORES * width, width)]
        high = gain[:, pl.ds((y * CORES + 1) * width, width)]
        scaled = (block * jnp.where(core == 0, low, high)).astype(bf16)
        start = pl.multiple_of((y * CORES + core) * width, width)
        own = own + jnp.dot(scaled, up[pl.ds(start, width), :], preferred_element_type=f32)
        other = other + jnp.dot(scaled, up_other[y], preferred_element_type=f32)
    partial[:, pl.ds(0, units)] = jnp.where(core == 0, own, other)
    partial[:, pl.ds(units, units)] = jnp.where(core == 0, other, own)
    total = jnp.sum(squares, axis=-1, keepdims=True)
    partial[:, pl.ds(CORES * units, HD)] = jnp.broadcast_to(total, (rows, HD))


def down_kernel(n_x, n_y, width_all, partials, down, down_other, half):
    f32, bf16 = jnp.float32, jnp.bfloat16
    core = lax.axis_index("core")
    units = down.shape[0]
    slots, width = half.shape[1:]
    squares = partials[0, :, pl.ds(CORES * units, HD)] + partials[1, :, pl.ds(CORES * units, HD)]
    inverse = lax.rsqrt(squares[:, :1] * (1.0 / width_all) + 1e-06)
    acts = []
    for c in range(CORES):
        cols = pl.ds(c * units, units)
        summed = (partials[0, :, cols] + partials[1, :, cols]) * inverse
        acts.append(jax.nn.gelu(summed).astype(bf16))
    own = jnp.where(core == 0, acts[0], acts[1])
    other = jnp.where(core == 0, acts[1], acts[0])
    for y in range(n_y):
        start = pl.multiple_of((y * CORES + core) * width, width)
        piece = jnp.dot(own, down[:, pl.ds(start, width)], preferred_element_type=f32)
        cols = pl.ds(y * width, width)
        piece = piece + jnp.dot(other, down_other[:, cols], preferred_element_type=f32)
        piece = piece.astype(bf16)
        for x in range(n_x):
            half[x * n_y + y] = piece[x * slots : (x + 1) * slots]


def held_in_vmem(*args):
    return [pltpu.with_memory_space_constraint(arg, pltpu.VMEM) for arg in args]


def run_units(n_x, n_y, plane, norm_gain, w_up, up_other):
    vmem = pl.BlockSpec(memory_space=pltpu.VMEM)
    shape = (n_x * plane.shape[1], CORES * w_up.shape[1] + HD)
    return pl.pallas_call(
        functools.partial(units_kernel, n_x, n_y),
        out_shape=in_vmem(shape, jnp.float32),
        in_specs=[vmem] * 4,
        out_specs=vmem,
        name="units",
    )(*held_in_vmem(plane, norm_gain[None, :], w_up, up_other))


def run_down(n_x, n_y, width_all, shape, partials, w_down, down_other):
    vmem = pl.BlockSpec(memory_space=pltpu.VMEM)
    return pl.pallas_call(
        functools.partial(down_kernel, n_x, n_y, width_all),
        out_shape=in_vmem(shape, jnp.bfloat16),
        in_specs=[vmem] * 3,
        out_specs=vmem,
        name="down",
    )(*held_in_vmem(partials, w_down, down_other))


def on_device(
    queries,
    new_keys,
    new_values,
    key_cache,
    value_cache,
    lengths,
    resid,
    norm_gain,
    w_out,
    experts,
    w_up,
    w_down,
):
    bf16, f32 = jnp.bfloat16, jnp.float32
    count, width_all = resid.shape
    n_z, n_x, n_y = lax.axis_size("z"), lax.axis_size("x"), lax.axis_size("y")
    width = width_all // (n_y * CORES)
    core = lax.axis_index("core")

    slots = n_z * SLOTS
    keep, give, table = attend(
        n_y,
        slots,
        queries,
        new_keys,
        new_values,
        key_cache,
        value_cache,
        lengths,
        resid,
        w_out,
        experts[:, 0],
    )
    given = lax.all_gather(give, "core", axis=0)
    chip = keep + lax.dynamic_index_in_dim(given, 1 - core, 0, keepdims=False)
    chip = chip.astype(bf16).reshape(count, n_y, width)
    packed = jnp.einsum("sr,ryc->syc", table, chip, preferred_element_type=f32)
    packed = packed.astype(bf16).reshape(n_z, SLOTS, n_y, width).transpose(0, 2, 1, 3)
    packed = packed.reshape(n_z * n_y, SLOTS, width)
    packed, up, down = lax.optimization_barrier((packed, w_up[0], w_down[0]))
    swap = [(0, 1), (1, 0)]
    up_give = up.reshape(n_y, CORES, width, up.shape[1])
    up_give = lax.dynamic_index_in_dim(up_give, 1 - core, 1, keepdims=False)
    up_other = lax.ppermute(up_give, "core", swap)
    down_give = down.reshape(down.shape[0], n_y, CORES, width)
    down_give = lax.dynamic_index_in_dim(down_give, 1 - core, 2, keepdims=False)
    down_other = lax.ppermute(down_give.reshape(down.shape[0], n_y * width), "core", swap)
    got = lax.all_to_all(packed, ("z", "y"), split_axis=0, concat_axis=0, tiled=True)
    hidden = jnp.sum(got.reshape(n_z, n_y, SLOTS, width).astype(f32), axis=1).reshape(slots, width)

    spread = jnp.broadcast_to(hidden.astype(bf16)[None], (n_x * n_y, slots, width))
    plane = lax.all_to_all(spread, ("x", "y"), split_axis=0, concat_axis=0, tiled=True)
    partial = run_units(n_x, n_y, plane, norm_gain, up, up_other)
    partials = lax.all_gather(partial, "core", axis=0)
    half = run_down(n_x, n_y, width_all, plane.shape, partials, down, down_other)
    parts = lax.all_to_all(half, ("x", "y"), split_axis=0, concat_axis=0, tiled=True)
    mixed = (hidden + jnp.sum(parts.astype(f32), axis=0)).astype(bf16)
    back = lax.all_to_all(
        mixed.reshape(n_z, SLOTS, width), "z", split_axis=0, concat_axis=0, tiled=True
    )
    back = back.reshape(slots, width)
    out = jnp.einsum("sr,sc->rc", table, back, preferred_element_type=f32)
    return out.astype(bf16)


def solution(mesh):
    n_x = GROUP
    n_z = mesh.shape["dp"] // n_x
    n_y = mesh.shape["cuts"] // CORES
    fine = Mesh(mesh.devices.reshape(n_z, n_x, n_y, CORES), ("z", "x", "y", "core"))
    rows, cols = ("z", "x"), ("y", "core")
    placed = (
        P(rows, cols),
        P(rows, cols),
        P(rows, cols),
        P(rows, None, cols),
        P(rows, None, cols),
        P(rows),
        P(rows, None),
        P(),
        P(cols, None),
        P(rows, None),
        P(rows, None, cols),
        P(rows, cols, None),
    )
    return jax.shard_map(
        on_device, mesh=fine, in_specs=placed, out_specs=P(rows, cols), check_vma=False
    )
```

```python
import functools

import jax
import jax.numpy as jnp
from jax import lax
from jax.experimental import pallas as pl
from jax.experimental.pallas import tpu as pltpu
from jax.sharding import Mesh
from jax.sharding import PartitionSpec as P

HD = 128
GROUP = 4
CORES = 2
SLOTS = 2


def in_vmem(shape, dtype):
    return pltpu.VMEM(shape, dtype)


def attend_kernel(n_y, *refs):
    f32, bf16 = jnp.float32, jnp.bfloat16
    sources, (keep, give, table), held, sems = refs[:9], refs[9:12], refs[12:21], refs[21]
    core, my_y = lax.axis_index("core"), lax.axis_index("y")
    copies = [
        pltpu.make_async_copy(source, target, sems.at[i])
        for i, (source, target) in enumerate(zip(sources, held))
    ]
    for copy in copies:
        copy.start()
    lengths, ids, queries, key_cache, new_keys, value_cache, new_values, w_out, resid = held
    count, feats = queries.shape
    spots = key_cache.shape[0]
    length = spots // count
    scale = 1.0 / HD**0.5
    for copy in copies[:2]:
        copy.wait()
    row = lax.broadcasted_iota(jnp.int32, (count, spots), 0)
    spot = lax.broadcasted_iota(jnp.int32, (count, spots), 1)
    limit = jnp.zeros((count, spots), jnp.int32)
    for r in range(count):
        limit = jnp.where(row == r, r * length + lengths[r], limit)
    valid = (spot >= row * length) & (spot < limit)
    slot = lax.broadcasted_iota(jnp.int32, table.shape, 0)
    name = lax.broadcasted_iota(jnp.int32, table.shape, 1)
    hot = jnp.zeros(table.shape, f32)
    for r in range(count):
        place = ids[r] * SLOTS
        for q in range(r):
            place = place + (ids[q] == ids[r]).astype(jnp.int32)
        hot = jnp.where((name == r) & (slot == place), 1.0, hot)
    table[...] = hot.astype(bf16)
    for copy in copies[2:5]:
        copy.wait()
    probs = []
    for h in range(feats // HD):
        cols = slice(h * HD, (h + 1) * HD)
        query = queries[:, cols]
        scores = lax.dot_general(
            query, key_cache[:, cols], (((1,), (1,)), ((), ())), preferred_element_type=f32
        )
        scores = jnp.where(valid, scores * scale, -1e30)
        fresh = query.astype(f32) * new_keys[:, cols].astype(f32)
        fresh = jnp.sum(fresh, axis=-1, keepdims=True) * scale
        peak = jnp.maximum(jnp.max(scores, axis=-1, keepdims=True), fresh)
        pcache = jnp.where(valid, jnp.exp(scores - peak), 0.0)
        pnew = jnp.exp(fresh - peak)
        total = jnp.sum(pcache, axis=-1, keepdims=True) + pnew
        probs.append(((pcache / total).astype(bf16), (pnew / total).astype(bf16).astype(f32)))
    for copy in copies[5:7]:
        copy.wait()
    heads = []
    for h, (pcache, pnew) in enumerate(probs):
        cols = slice(h * HD, (h + 1) * HD)
        summed = jnp.dot(pcache, value_cache[:, cols], preferred_element_type=f32)
        summed = summed + pnew * new_values[:, cols].astype(f32)
        heads.append(summed.astype(bf16))
    heads_out = jnp.concatenate(heads, axis=1)
    for copy in copies[7:]:
        copy.wait()
    width = w_out.shape[1] // (n_y * CORES)
    for y in range(n_y):
        pair = []
        for c in range(CORES):
            cols = pl.ds((y * CORES + c) * width, width)
            pair.append(jnp.dot(heads_out, w_out[:, cols], preferred_element_type=f32))
        low = resid[:, pl.ds(y * CORES * width, width)].astype(f32)
        high = resid[:, pl.ds((y * CORES + 1) * width, width)].astype(f32)
        rest = jnp.where(my_y == y, jnp.where(core == 0, low, high), 0.0)
        keep[:, pl.ds(y * width, width)] = jnp.where(core == 0, pair[0], pair[1]) + rest
        give[:, pl.ds(y * width, width)] = jnp.where(core == 0, pair[1], pair[0])


def attend(
    n_y,
    slots,
    queries,
    new_keys,
    new_values,
    key_cache,
    value_cache,
    lengths,
    resid,
    w_out,
    ids,
):
    count, feats = queries.shape
    spots = count * key_cache.shape[1]
    args = (
        lengths,
        ids,
        queries,
        key_cache.reshape(spots, feats),
        new_keys,
        value_cache.reshape(spots, feats),
        new_values,
        w_out,
        resid,
    )
    half = in_vmem((count, w_out.shape[1] // CORES), jnp.float32)
    vmem, anywhere = pl.BlockSpec(memory_space=pltpu.VMEM), pl.BlockSpec(memory_space=pl.ANY)
    spaces = [pltpu.SMEM] * 2 + [pltpu.VMEM] * 7
    return pl.pallas_call(
        functools.partial(attend_kernel, n_y),
        out_shape=(half, half, in_vmem((slots, count), jnp.bfloat16)),
        in_specs=[anywhere] * len(args),
        out_specs=(vmem,) * 3,
        scratch_shapes=[space(arg.shape, arg.dtype) for space, arg in zip(spaces, args)]
        + [pltpu.SemaphoreType.DMA((len(args),))],
        name="attend",
    )(*args)


def expert_kernel(n_x, n_y, pair, gain, up, down, keep, give):
    f32, bf16 = jnp.float32, jnp.bfloat16
    core = lax.axis_index("core")
    slots, width = pair.shape[2:]
    width_all = n_y * CORES * width
    rows = n_x * slots
    squares = jnp.zeros((rows, width), f32)
    units = jnp.zeros((rows, up.shape[1]), f32)
    for y in range(n_y):
        for c in range(CORES):
            cols = pl.ds((y * CORES + c) * width, width)
            block = [pair[c, x * n_y + y] for x in range(n_x)]
            block = jnp.concatenate(block, axis=0).astype(f32)
            squares = squares + block * block
            scaled = (block * gain[:, cols]).astype(bf16)
            units = units + jnp.dot(scaled, up[cols, :], preferred_element_type=f32)
    meansq = jnp.sum(squares, axis=-1, keepdims=True) * (1.0 / width_all)
    units = units * lax.rsqrt(meansq + 1e-06)
    act = jax.nn.gelu(units).astype(bf16)
    for y in range(n_y):
        both = []
        for c in range(CORES):
            cols = pl.ds((y * CORES + c) * width, width)
            both.append(jnp.dot(act, down[:, cols], preferred_element_type=f32))
        own = jnp.where(core == 0, both[0], both[1])
        other = jnp.where(core == 0, both[1], both[0]).astype(bf16)
        for x in range(n_x):
            keep[x * n_y + y] = own[x * slots : (x + 1) * slots]
            give[x * n_y + y] = other[x * slots : (x + 1) * slots]


def run_expert(n_x, n_y, pair, norm_gain, w_up, w_down):
    vmem = pl.BlockSpec(memory_space=pltpu.VMEM)
    args = [
        pltpu.with_memory_space_constraint(arg, pltpu.VMEM)
        for arg in (pair, norm_gain[None, :], w_up, w_down)
    ]
    return pl.pallas_call(
        functools.partial(expert_kernel, n_x, n_y),
        out_shape=(
            in_vmem(pair.shape[1:], jnp.float32),
            in_vmem(pair.shape[1:], jnp.bfloat16),
        ),
        in_specs=[vmem] * 4,
        out_specs=(vmem, vmem),
        name="expert",
    )(*args)


def on_device(
    queries,
    new_keys,
    new_values,
    key_cache,
    value_cache,
    lengths,
    resid,
    norm_gain,
    w_out,
    experts,
    w_up,
    w_down,
):
    bf16, f32 = jnp.bfloat16, jnp.float32
    count, width_all = resid.shape
    n_z, n_x, n_y = lax.axis_size("z"), lax.axis_size("x"), lax.axis_size("y")
    width = width_all // (n_y * CORES)
    core = lax.axis_index("core")

    slots = n_z * SLOTS
    keep, give, table = attend(
        n_y,
        slots,
        queries,
        new_keys,
        new_values,
        key_cache,
        value_cache,
        lengths,
        resid,
        w_out,
        experts[:, 0],
    )
    given = lax.all_gather(give, "core", axis=0)
    chip = keep + lax.dynamic_index_in_dim(given, 1 - core, 0, keepdims=False)
    chip = chip.astype(bf16).reshape(count, n_y, width)
    packed = jnp.einsum("sr,ryc->syc", table, chip, preferred_element_type=f32)
    packed = packed.astype(bf16).reshape(n_z, SLOTS, n_y, width).transpose(0, 2, 1, 3)
    packed = packed.reshape(n_z * n_y, SLOTS, width)
    got = lax.all_to_all(packed, ("z", "y"), split_axis=0, concat_axis=0, tiled=True)
    hidden = jnp.sum(got.reshape(n_z, n_y, SLOTS, width).astype(f32), axis=1).reshape(slots, width)

    spread = jnp.broadcast_to(hidden.astype(bf16)[None], (n_x * n_y, slots, width))
    plane = lax.all_to_all(spread, ("x", "y"), split_axis=0, concat_axis=0, tiled=True)
    pair = lax.all_gather(plane, "core", axis=0)
    keep, give = run_expert(n_x, n_y, pair, norm_gain, w_up[0], w_down[0])
    given = lax.all_gather(give, "core", axis=0)
    half = keep + lax.dynamic_index_in_dim(given, 1 - core, 0, keepdims=False).astype(f32)
    half = half.astype(bf16)
    parts = lax.all_to_all(half, ("x", "y"), split_axis=0, concat_axis=0, tiled=True)
    mixed = (hidden + jnp.sum(parts.astype(f32), axis=0)).astype(bf16)
    back = lax.all_to_all(
        mixed.reshape(n_z, SLOTS, width), "z", split_axis=0, concat_axis=0, tiled=True
    )
    back = back.reshape(slots, width)
    out = jnp.einsum("sr,sc->rc", table, back, preferred_element_type=f32)
    return out.astype(bf16)


def solution(mesh):
    n_x = GROUP
    n_z = mesh.shape["dp"] // n_x
    n_y = mesh.shape["cuts"] // CORES
    fine = Mesh(mesh.devices.reshape(n_z, n_x, n_y, CORES), ("z", "x", "y", "core"))
    rows, cols = ("z", "x"), ("y", "core")
    placed = (
        P(rows, cols),
        P(rows, cols),
        P(rows, cols),
        P(rows, None, cols),
        P(rows, None, cols),
        P(rows),
        P(rows, None),
        P(),
        P(cols, None),
        P(rows, None),
        P(rows, None, cols),
        P(rows, cols, None),
    )
    return jax.shard_map(
        on_device, mesh=fine, in_specs=placed, out_specs=P(rows, cols), check_vma=False
    )
```

```python
import functools

import jax
import jax.numpy as jnp
from jax import lax
from jax.experimental import pallas as pl
from jax.experimental.pallas import tpu as pltpu
from jax.sharding import Mesh
from jax.sharding import PartitionSpec as P

HD = 128
GROUP = 4
CORES = 2
SLOTS = 2


def in_vmem(shape, dtype):
    return pltpu.VMEM(shape, dtype)


def attend_kernel(n_y, *refs):
    f32, bf16 = jnp.float32, jnp.bfloat16
    sources, (keep, give, table), held, sems = refs[:9], refs[9:12], refs[12:21], refs[21]
    core, my_y = lax.axis_index("core"), lax.axis_index("y")
    copies = [
        pltpu.make_async_copy(source, target, sems.at[i])
        for i, (source, target) in enumerate(zip(sources, held))
    ]
    for copy in copies:
        copy.start()
    lengths, ids, queries, key_cache, new_keys, value_cache, new_values, w_out, resid = held
    count, feats = queries.shape
    spots = key_cache.shape[0]
    length = spots // count
    scale = 1.0 / HD**0.5
    for copy in copies[:2]:
        copy.wait()
    row = lax.broadcasted_iota(jnp.int32, (count, spots), 0)
    spot = lax.broadcasted_iota(jnp.int32, (count, spots), 1)
    limit = jnp.zeros((count, spots), jnp.int32)
    for r in range(count):
        limit = jnp.where(row == r, r * length + lengths[r], limit)
    valid = (spot >= row * length) & (spot < limit)
    slot = lax.broadcasted_iota(jnp.int32, table.shape, 0)
    name = lax.broadcasted_iota(jnp.int32, table.shape, 1)
    hot = jnp.zeros(table.shape, f32)
    for r in range(count):
        place = ids[r] * SLOTS
        for q in range(r):
            place = place + (ids[q] == ids[r]).astype(jnp.int32)
        hot = jnp.where((name == r) & (slot == place), 1.0, hot)
    table[...] = hot.astype(bf16)
    for copy in copies[2:5]:
        copy.wait()
    probs = []
    for h in range(feats // HD):
        cols = slice(h * HD, (h + 1) * HD)
        query = queries[:, cols]
        scores = lax.dot_general(
            query, key_cache[:, cols], (((1,), (1,)), ((), ())), preferred_element_type=f32
        )
        scores = jnp.where(valid, scores * scale, -1e30)
        fresh = query.astype(f32) * new_keys[:, cols].astype(f32)
        fresh = jnp.sum(fresh, axis=-1, keepdims=True) * scale
        peak = jnp.maximum(jnp.max(scores, axis=-1, keepdims=True), fresh)
        pcache = jnp.where(valid, jnp.exp(scores - peak), 0.0)
        pnew = jnp.exp(fresh - peak)
        total = jnp.sum(pcache, axis=-1, keepdims=True) + pnew
        probs.append(((pcache / total).astype(bf16), (pnew / total).astype(bf16).astype(f32)))
    for copy in copies[5:7]:
        copy.wait()
    heads = []
    for h, (pcache, pnew) in enumerate(probs):
        cols = slice(h * HD, (h + 1) * HD)
        summed = jnp.dot(pcache, value_cache[:, cols], preferred_element_type=f32)
        summed = summed + pnew * new_values[:, cols].astype(f32)
        heads.append(summed.astype(bf16))
    heads_out = jnp.concatenate(heads, axis=1)
    for copy in copies[7:]:
        copy.wait()
    width = w_out.shape[1] // (n_y * CORES)
    for y in range(n_y):
        pair = []
        for c in range(CORES):
            cols = pl.ds((y * CORES + c) * width, width)
            pair.append(jnp.dot(heads_out, w_out[:, cols], preferred_element_type=f32))
        low = resid[:, pl.ds(y * CORES * width, width)].astype(f32)
        high = resid[:, pl.ds((y * CORES + 1) * width, width)].astype(f32)
        rest = jnp.where(my_y == y, jnp.where(core == 0, low, high), 0.0)
        keep[:, pl.ds(y * width, width)] = jnp.where(core == 0, pair[0], pair[1]) + rest
        give[:, pl.ds(y * width, width)] = jnp.where(core == 0, pair[1], pair[0])


def attend(
    n_y,
    slots,
    queries,
    new_keys,
    new_values,
    key_cache,
    value_cache,
    lengths,
    resid,
    w_out,
    ids,
):
    count, feats = queries.shape
    spots = count * key_cache.shape[1]
    args = (
        lengths,
        ids,
        queries,
        key_cache.reshape(spots, feats),
        new_keys,
        value_cache.reshape(spots, feats),
        new_values,
        w_out,
        resid,
    )
    half = in_vmem((count, w_out.shape[1] // CORES), jnp.float32)
    vmem, anywhere = pl.BlockSpec(memory_space=pltpu.VMEM), pl.BlockSpec(memory_space=pl.ANY)
    spaces = [pltpu.SMEM] * 2 + [pltpu.VMEM] * 7
    return pl.pallas_call(
        functools.partial(attend_kernel, n_y),
        out_shape=(half, half, in_vmem((slots, count), jnp.bfloat16)),
        in_specs=[anywhere] * len(args),
        out_specs=(vmem,) * 3,
        scratch_shapes=[space(arg.shape, arg.dtype) for space, arg in zip(spaces, args)]
        + [pltpu.SemaphoreType.DMA((len(args),))],
        name="attend",
    )(*args)


def expert_kernel(n_x, n_y, pair, gain, up, down, keep, give):
    f32, bf16 = jnp.float32, jnp.bfloat16
    core = lax.axis_index("core")
    slots, width = pair.shape[2:]
    width_all = n_y * CORES * width
    rows = n_x * slots
    squares = jnp.zeros((rows, width), f32)
    units = jnp.zeros((rows, up.shape[1]), f32)
    for y in range(n_y):
        for c in range(CORES):
            cols = pl.ds((y * CORES + c) * width, width)
            block = [pair[c, x * n_y + y] for x in range(n_x)]
            block = jnp.concatenate(block, axis=0).astype(f32)
            squares = squares + block * block
            scaled = (block * gain[:, cols]).astype(bf16)
            units = units + jnp.dot(scaled, up[cols, :], preferred_element_type=f32)
    meansq = jnp.sum(squares, axis=-1, keepdims=True) * (1.0 / width_all)
    units = units * lax.rsqrt(meansq + 1e-06)
    act = jax.nn.gelu(units).astype(bf16)
    for y in range(n_y):
        both = []
        for c in range(CORES):
            cols = pl.ds((y * CORES + c) * width, width)
            both.append(jnp.dot(act, down[:, cols], preferred_element_type=f32))
        own = jnp.where(core == 0, both[0], both[1])
        other = jnp.where(core == 0, both[1], both[0]).astype(bf16)
        for x in range(n_x):
            keep[x * n_y + y] = own[x * slots : (x + 1) * slots]
            give[x * n_y + y] = other[x * slots : (x + 1) * slots]


def run_expert(n_x, n_y, pair, norm_gain, w_up, w_down):
    vmem = pl.BlockSpec(memory_space=pltpu.VMEM)
    args = [
        pltpu.with_memory_space_constraint(arg, pltpu.VMEM)
        for arg in (pair, norm_gain[None, :], w_up, w_down)
    ]
    return pl.pallas_call(
        functools.partial(expert_kernel, n_x, n_y),
        out_shape=(
            in_vmem(pair.shape[1:], jnp.float32),
            in_vmem(pair.shape[1:], jnp.bfloat16),
        ),
        in_specs=[vmem] * 4,
        out_specs=(vmem, vmem),
        name="expert",
    )(*args)


def on_device(
    queries,
    new_keys,
    new_values,
    key_cache,
    value_cache,
    lengths,
    resid,
    norm_gain,
    w_out,
    experts,
    w_up,
    w_down,
):
    bf16, f32 = jnp.bfloat16, jnp.float32
    count, width_all = resid.shape
    n_z, n_x, n_y = lax.axis_size("z"), lax.axis_size("x"), lax.axis_size("y")
    width = width_all // (n_y * CORES)
    core = lax.axis_index("core")

    slots = n_z * SLOTS
    keep, give, table = attend(
        n_y,
        slots,
        queries,
        new_keys,
        new_values,
        key_cache,
        value_cache,
        lengths,
        resid,
        w_out,
        experts[:, 0],
    )
    given = lax.all_gather(give, "core", axis=0)
    chip = keep + lax.dynamic_index_in_dim(given, 1 - core, 0, keepdims=False)
    chip = chip.astype(bf16).reshape(count, n_y, width)
    packed = jnp.einsum("sr,ryc->ysc", table, chip, preferred_element_type=f32)
    packed = packed.astype(bf16).reshape(n_y * n_z, SLOTS, width)
    got = lax.all_to_all(packed, ("y", "z"), split_axis=0, concat_axis=0, tiled=True)
    hidden = jnp.sum(got.reshape(n_y, slots, width).astype(f32), axis=0)

    spread = jnp.broadcast_to(hidden.astype(bf16)[None], (n_x * n_y, slots, width))
    plane = lax.all_to_all(spread, ("x", "y"), split_axis=0, concat_axis=0, tiled=True)
    pair = lax.all_gather(plane, "core", axis=0)
    keep, give = run_expert(n_x, n_y, pair, norm_gain, w_up[0], w_down[0])
    given = lax.all_gather(give, "core", axis=0)
    half = keep + lax.dynamic_index_in_dim(given, 1 - core, 0, keepdims=False).astype(f32)
    half = half.astype(bf16)
    parts = lax.all_to_all(half, ("x", "y"), split_axis=0, concat_axis=0, tiled=True)
    mixed = (hidden + jnp.sum(parts.astype(f32), axis=0)).astype(bf16)
    back = lax.all_to_all(
        mixed.reshape(n_z, SLOTS, width), "z", split_axis=0, concat_axis=0, tiled=True
    )
    back = back.reshape(slots, width)
    out = jnp.einsum("sr,sc->rc", table, back, preferred_element_type=f32)
    return out.astype(bf16)


def solution(mesh):
    n_x = GROUP
    n_z = mesh.shape["dp"] // n_x
    n_y = mesh.shape["cuts"] // CORES
    fine = Mesh(mesh.devices.reshape(n_z, n_x, n_y, CORES), ("z", "x", "y", "core"))
    rows, cols = ("z", "x"), ("y", "core")
    placed = (
        P(rows, cols),
        P(rows, cols),
        P(rows, cols),
        P(rows, None, cols),
        P(rows, None, cols),
        P(rows),
        P(rows, None),
        P(),
        P(cols, None),
        P(rows, None),
        P(rows, None, cols),
        P(rows, cols, None),
    )
    return jax.shard_map(
        on_device, mesh=fine, in_specs=placed, out_specs=P(rows, cols), check_vma=False
    )
```

```python
import functools

import jax
import jax.numpy as jnp
from jax import lax
from jax.experimental import pallas as pl
from jax.experimental.pallas import tpu as pltpu
from jax.sharding import Mesh
from jax.sharding import PartitionSpec as P

HD = 128
GROUP = 4
CORES = 2
SLOTS = 2


def in_vmem(shape, dtype):
    return pltpu.VMEM(shape, dtype)


def attend_kernel(n_y, *refs):
    f32, bf16 = jnp.float32, jnp.bfloat16
    sources, (keep, give, table, mask), held, sems = refs[:9], refs[9:13], refs[13:22], refs[22]
    core, my_y = lax.axis_index("core"), lax.axis_index("y")
    copies = [
        pltpu.make_async_copy(source, target, sems.at[i])
        for i, (source, target) in enumerate(zip(sources, held))
    ]
    for copy in copies:
        copy.start()
    lengths, ids, queries, key_cache, new_keys, value_cache, new_values, w_out, resid = held
    count, feats = queries.shape
    spots = key_cache.shape[0]
    length = spots // count
    scale = 1.0 / HD**0.5
    for copy in copies[:2]:
        copy.wait()
    row = lax.broadcasted_iota(jnp.int32, (count, spots), 0)
    spot = lax.broadcasted_iota(jnp.int32, (count, spots), 1)
    limit = jnp.zeros((count, spots), jnp.int32)
    for r in range(count):
        limit = jnp.where(row == r, r * length + lengths[r], limit)
    valid = (spot >= row * length) & (spot < limit)
    slot = lax.broadcasted_iota(jnp.int32, table.shape, 0)
    name = lax.broadcasted_iota(jnp.int32, table.shape, 1)
    hot = jnp.zeros(table.shape, f32)
    for r in range(count):
        place = ids[r] * SLOTS
        for q in range(r):
            place = place + (ids[q] == ids[r]).astype(jnp.int32)
        hot = jnp.where((name == r) & (slot == place), 1.0, hot)
    table[...] = hot.astype(bf16)
    mask[...] = hot
    for copy in copies[2:5]:
        copy.wait()
    probs = []
    for h in range(feats // HD):
        cols = slice(h * HD, (h + 1) * HD)
        query = queries[:, cols]
        scores = lax.dot_general(
            query, key_cache[:, cols], (((1,), (1,)), ((), ())), preferred_element_type=f32
        )
        scores = jnp.where(valid, scores * scale, -1e30)
        fresh = query.astype(f32) * new_keys[:, cols].astype(f32)
        fresh = jnp.sum(fresh, axis=-1, keepdims=True) * scale
        peak = jnp.maximum(jnp.max(scores, axis=-1, keepdims=True), fresh)
        pcache = jnp.where(valid, jnp.exp(scores - peak), 0.0)
        pnew = jnp.exp(fresh - peak)
        total = jnp.sum(pcache, axis=-1, keepdims=True) + pnew
        probs.append(((pcache / total).astype(bf16), (pnew / total).astype(bf16).astype(f32)))
    for copy in copies[5:7]:
        copy.wait()
    heads = []
    for h, (pcache, pnew) in enumerate(probs):
        cols = slice(h * HD, (h + 1) * HD)
        summed = jnp.dot(pcache, value_cache[:, cols], preferred_element_type=f32)
        summed = summed + pnew * new_values[:, cols].astype(f32)
        heads.append(summed.astype(bf16))
    heads_out = jnp.concatenate(heads, axis=1)
    for copy in copies[7:]:
        copy.wait()
    width = w_out.shape[1] // (n_y * CORES)
    for y in range(n_y):
        pair = []
        for c in range(CORES):
            cols = pl.ds((y * CORES + c) * width, width)
            pair.append(jnp.dot(heads_out, w_out[:, cols], preferred_element_type=f32))
        low = resid[:, pl.ds(y * CORES * width, width)].astype(f32)
        high = resid[:, pl.ds((y * CORES + 1) * width, width)].astype(f32)
        rest = jnp.where(my_y == y, jnp.where(core == 0, low, high), 0.0)
        keep[:, pl.ds(y * width, width)] = jnp.where(core == 0, pair[0], pair[1]) + rest
        give[:, pl.ds(y * width, width)] = jnp.where(core == 0, pair[1], pair[0])


def attend(
    n_y,
    slots,
    queries,
    new_keys,
    new_values,
    key_cache,
    value_cache,
    lengths,
    resid,
    w_out,
    ids,
):
    count, feats = queries.shape
    spots = count * key_cache.shape[1]
    args = (
        lengths,
        ids,
        queries,
        key_cache.reshape(spots, feats),
        new_keys,
        value_cache.reshape(spots, feats),
        new_values,
        w_out,
        resid,
    )
    half = in_vmem((count, w_out.shape[1] // CORES), jnp.float32)
    vmem, anywhere = pl.BlockSpec(memory_space=pltpu.VMEM), pl.BlockSpec(memory_space=pl.ANY)
    spaces = [pltpu.SMEM] * 2 + [pltpu.VMEM] * 7
    return pl.pallas_call(
        functools.partial(attend_kernel, n_y),
        out_shape=(
            half,
            half,
            in_vmem((slots, count), jnp.bfloat16),
            in_vmem((slots, count), jnp.float32),
        ),
        in_specs=[anywhere] * len(args),
        out_specs=(vmem,) * 4,
        scratch_shapes=[space(arg.shape, arg.dtype) for space, arg in zip(spaces, args)]
        + [pltpu.SemaphoreType.DMA((len(args),))],
        name="attend",
    )(*args)


def expert_kernel(n_x, n_y, pair, gain, up, down, keep, give):
    f32, bf16 = jnp.float32, jnp.bfloat16
    core = lax.axis_index("core")
    slots, width = pair.shape[2:]
    width_all = n_y * CORES * width
    rows = n_x * slots
    squares = jnp.zeros((rows, width), f32)
    units = jnp.zeros((rows, up.shape[1]), f32)
    for y in range(n_y):
        for c in range(CORES):
            cols = pl.ds((y * CORES + c) * width, width)
            block = [pair[c, x * n_y + y] for x in range(n_x)]
            block = jnp.concatenate(block, axis=0).astype(f32)
            squares = squares + block * block
            scaled = (block * gain[:, cols]).astype(bf16)
            units = units + jnp.dot(scaled, up[cols, :], preferred_element_type=f32)
    meansq = jnp.sum(squares, axis=-1, keepdims=True) * (1.0 / width_all)
    units = units * lax.rsqrt(meansq + 1e-06)
    act = jax.nn.gelu(units).astype(bf16)
    for y in range(n_y):
        both = []
        for c in range(CORES):
            cols = pl.ds((y * CORES + c) * width, width)
            both.append(jnp.dot(act, down[:, cols], preferred_element_type=f32))
        own = jnp.where(core == 0, both[0], both[1])
        other = jnp.where(core == 0, both[1], both[0]).astype(bf16)
        for x in range(n_x):
            keep[x * n_y + y] = own[x * slots : (x + 1) * slots]
            give[x * n_y + y] = other[x * slots : (x + 1) * slots]


def run_expert(n_x, n_y, pair, norm_gain, w_up, w_down):
    vmem = pl.BlockSpec(memory_space=pltpu.VMEM)
    args = [
        pltpu.with_memory_space_constraint(arg, pltpu.VMEM)
        for arg in (pair, norm_gain[None, :], w_up, w_down)
    ]
    return pl.pallas_call(
        functools.partial(expert_kernel, n_x, n_y),
        out_shape=(
            in_vmem(pair.shape[1:], jnp.float32),
            in_vmem(pair.shape[1:], jnp.bfloat16),
        ),
        in_specs=[vmem] * 4,
        out_specs=(vmem, vmem),
        name="expert",
    )(*args)


def on_device(
    queries,
    new_keys,
    new_values,
    key_cache,
    value_cache,
    lengths,
    resid,
    norm_gain,
    w_out,
    experts,
    w_up,
    w_down,
):
    bf16, f32 = jnp.bfloat16, jnp.float32
    count, width_all = resid.shape
    n_z, n_x, n_y = lax.axis_size("z"), lax.axis_size("x"), lax.axis_size("y")
    width = width_all // (n_y * CORES)
    core = lax.axis_index("core")

    slots = n_z * SLOTS
    keep, give, table, mask = attend(
        n_y,
        slots,
        queries,
        new_keys,
        new_values,
        key_cache,
        value_cache,
        lengths,
        resid,
        w_out,
        experts[:, 0],
    )
    given = lax.all_gather(give, "core", axis=0)
    chip = keep + lax.dynamic_index_in_dim(given, 1 - core, 0, keepdims=False)
    chip = chip.astype(bf16).reshape(count, n_y, width)
    packed = jnp.einsum("sr,ryc->ysc", table, chip, preferred_element_type=f32)
    packed = packed.astype(bf16).reshape(n_y * n_z, SLOTS, width)
    got = lax.all_to_all(packed, ("y", "z"), split_axis=0, concat_axis=0, tiled=True)
    hidden = jnp.sum(got.reshape(n_y, slots, width).astype(f32), axis=0)

    spread = jnp.broadcast_to(hidden.astype(bf16)[None], (n_x * n_y, slots, width))
    plane = lax.all_to_all(spread, ("x", "y"), split_axis=0, concat_axis=0, tiled=True)
    pair = lax.all_gather(plane, "core", axis=0)
    keep, give = run_expert(n_x, n_y, pair, norm_gain, w_up[0], w_down[0])
    given = lax.all_gather(give, "core", axis=0)
    half = keep + lax.dynamic_index_in_dim(given, 1 - core, 0, keepdims=False).astype(f32)
    half = half.astype(bf16)
    parts = lax.all_to_all(half, ("x", "y"), split_axis=0, concat_axis=0, tiled=True)
    mixed = (hidden + jnp.sum(parts.astype(f32), axis=0)).astype(bf16)
    back = lax.all_to_all(
        mixed.reshape(n_z, SLOTS, width), "z", split_axis=0, concat_axis=0, tiled=True
    )
    back = back.reshape(slots, 1, width).astype(f32)
    return jnp.sum(mask[:, :, None] * back, axis=0).astype(bf16)


def solution(mesh):
    n_x = GROUP
    n_z = mesh.shape["dp"] // n_x
    n_y = mesh.shape["cuts"] // CORES
    fine = Mesh(mesh.devices.reshape(n_z, n_x, n_y, CORES), ("z", "x", "y", "core"))
    rows, cols = ("z", "x"), ("y", "core")
    placed = (
        P(rows, cols),
        P(rows, cols),
        P(rows, cols),
        P(rows, None, cols),
        P(rows, None, cols),
        P(rows),
        P(rows, None),
        P(),
        P(cols, None),
        P(rows, None),
        P(rows, None, cols),
        P(rows, cols, None),
    )
    return jax.shard_map(
        on_device, mesh=fine, in_specs=placed, out_specs=P(rows, cols), check_vma=False
    )
```

```python
import functools

import jax
import jax.numpy as jnp
from jax import lax
from jax.experimental import pallas as pl
from jax.experimental.pallas import tpu as pltpu
from jax.sharding import Mesh
from jax.sharding import PartitionSpec as P

HD = 128
GROUP = 4
CORES = 2
SLOTS = 2


def in_vmem(shape, dtype):
    return pltpu.VMEM(shape, dtype)


def attend_kernel(n_y, *refs):
    f32, bf16 = jnp.float32, jnp.bfloat16
    sources, (keep, give, table, mask), held, sems = refs[:9], refs[9:13], refs[13:22], refs[22]
    core, my_y = lax.axis_index("core"), lax.axis_index("y")
    copies = [
        pltpu.make_async_copy(source, target, sems.at[i])
        for i, (source, target) in enumerate(zip(sources, held))
    ]
    for copy in copies:
        copy.start()
    lengths, ids, queries, key_cache, new_keys, value_cache, new_values, w_out, resid = held
    count, feats = queries.shape
    spots = key_cache.shape[0]
    length = spots // count
    scale = 1.0 / HD**0.5
    for copy in copies[:2]:
        copy.wait()
    row = lax.broadcasted_iota(jnp.int32, (count, spots), 0)
    spot = lax.broadcasted_iota(jnp.int32, (count, spots), 1)
    limit = jnp.zeros((count, spots), jnp.int32)
    for r in range(count):
        limit = jnp.where(row == r, r * length + lengths[r], limit)
    valid = (spot >= row * length) & (spot < limit)
    slot = lax.broadcasted_iota(jnp.int32, table.shape, 0)
    name = lax.broadcasted_iota(jnp.int32, table.shape, 1)
    hot = jnp.zeros(table.shape, f32)
    for r in range(count):
        place = ids[r] * SLOTS
        for q in range(r):
            place = place + (ids[q] == ids[r]).astype(jnp.int32)
        hot = jnp.where((name == r) & (slot == place), 1.0, hot)
    table[...] = hot.astype(bf16)
    mask[...] = hot
    for copy in copies[2:5]:
        copy.wait()
    probs = []
    for h in range(feats // HD):
        cols = slice(h * HD, (h + 1) * HD)
        query = queries[:, cols]
        scores = lax.dot_general(
            query, key_cache[:, cols], (((1,), (1,)), ((), ())), preferred_element_type=f32
        )
        scores = jnp.where(valid, scores * scale, -1e30)
        fresh = query.astype(f32) * new_keys[:, cols].astype(f32)
        fresh = jnp.sum(fresh, axis=-1, keepdims=True) * scale
        peak = jnp.maximum(jnp.max(scores, axis=-1, keepdims=True), fresh)
        pcache = jnp.where(valid, jnp.exp(scores - peak), 0.0)
        pnew = jnp.exp(fresh - peak)
        total = jnp.sum(pcache, axis=-1, keepdims=True) + pnew
        probs.append(((pcache / total).astype(bf16), (pnew / total).astype(bf16).astype(f32)))
    for copy in copies[5:7]:
        copy.wait()
    heads = []
    for h, (pcache, pnew) in enumerate(probs):
        cols = slice(h * HD, (h + 1) * HD)
        summed = jnp.dot(pcache, value_cache[:, cols], preferred_element_type=f32)
        summed = summed + pnew * new_values[:, cols].astype(f32)
        heads.append(summed.astype(bf16))
    heads_out = jnp.concatenate(heads, axis=1)
    for copy in copies[7:]:
        copy.wait()
    width = w_out.shape[1] // (n_y * CORES)
    for y in range(n_y):
        pair = []
        for c in range(CORES):
            cols = pl.ds((y * CORES + c) * width, width)
            pair.append(jnp.dot(heads_out, w_out[:, cols], preferred_element_type=f32))
        low = resid[:, pl.ds(y * CORES * width, width)].astype(f32)
        high = resid[:, pl.ds((y * CORES + 1) * width, width)].astype(f32)
        rest = jnp.where(my_y == y, jnp.where(core == 0, low, high), 0.0)
        keep[:, pl.ds(y * width, width)] = jnp.where(core == 0, pair[0], pair[1]) + rest
        give[:, pl.ds(y * width, width)] = jnp.where(core == 0, pair[1], pair[0])


def attend(
    n_y,
    slots,
    queries,
    new_keys,
    new_values,
    key_cache,
    value_cache,
    lengths,
    resid,
    w_out,
    ids,
):
    count, feats = queries.shape
    spots = count * key_cache.shape[1]
    args = (
        lengths,
        ids,
        queries,
        key_cache.reshape(spots, feats),
        new_keys,
        value_cache.reshape(spots, feats),
        new_values,
        w_out,
        resid,
    )
    half = in_vmem((count, w_out.shape[1] // CORES), jnp.float32)
    vmem, anywhere = pl.BlockSpec(memory_space=pltpu.VMEM), pl.BlockSpec(memory_space=pl.ANY)
    spaces = [pltpu.SMEM] * 2 + [pltpu.VMEM] * 7
    return pl.pallas_call(
        functools.partial(attend_kernel, n_y),
        out_shape=(
            half,
            half,
            in_vmem((slots, count), jnp.bfloat16),
            in_vmem((slots, count), jnp.float32),
        ),
        in_specs=[anywhere] * len(args),
        out_specs=(vmem,) * 4,
        scratch_shapes=[space(arg.shape, arg.dtype) for space, arg in zip(spaces, args)]
        + [pltpu.SemaphoreType.DMA((len(args),))],
        name="attend",
    )(*args)


def expert_kernel(n_x, n_y, pair, gain, up, down, keep, give):
    f32, bf16 = jnp.float32, jnp.bfloat16
    core = lax.axis_index("core")
    slots, width = pair.shape[2:]
    width_all = n_y * CORES * width
    rows = n_x * slots
    squares = jnp.zeros((rows, width), f32)
    units = jnp.zeros((rows, up.shape[1]), f32)
    for y in range(n_y):
        for c in range(CORES):
            cols = pl.ds((y * CORES + c) * width, width)
            block = [pair[c, y * n_x + x] for x in range(n_x)]
            block = jnp.concatenate(block, axis=0).astype(f32)
            squares = squares + block * block
            scaled = (block * gain[:, cols]).astype(bf16)
            units = units + jnp.dot(scaled, up[cols, :], preferred_element_type=f32)
    meansq = jnp.sum(squares, axis=-1, keepdims=True) * (1.0 / width_all)
    units = units * lax.rsqrt(meansq + 1e-06)
    act = jax.nn.gelu(units).astype(bf16)
    for y in range(n_y):
        both = []
        for c in range(CORES):
            cols = pl.ds((y * CORES + c) * width, width)
            both.append(jnp.dot(act, down[:, cols], preferred_element_type=f32))
        own = jnp.where(core == 0, both[0], both[1])
        other = jnp.where(core == 0, both[1], both[0]).astype(bf16)
        for x in range(n_x):
            keep[y * n_x + x] = own[x * slots : (x + 1) * slots]
            give[y * n_x + x] = other[x * slots : (x + 1) * slots]


def run_expert(n_x, n_y, pair, norm_gain, w_up, w_down):
    vmem = pl.BlockSpec(memory_space=pltpu.VMEM)
    args = [
        pltpu.with_memory_space_constraint(arg, pltpu.VMEM)
        for arg in (pair, norm_gain[None, :], w_up, w_down)
    ]
    return pl.pallas_call(
        functools.partial(expert_kernel, n_x, n_y),
        out_shape=(
            in_vmem(pair.shape[1:], jnp.float32),
            in_vmem(pair.shape[1:], jnp.bfloat16),
        ),
        in_specs=[vmem] * 4,
        out_specs=(vmem, vmem),
        name="expert",
    )(*args)


def on_device(
    queries,
    new_keys,
    new_values,
    key_cache,
    value_cache,
    lengths,
    resid,
    norm_gain,
    w_out,
    experts,
    w_up,
    w_down,
):
    bf16, f32 = jnp.bfloat16, jnp.float32
    count, width_all = resid.shape
    n_z, n_x, n_y = lax.axis_size("z"), lax.axis_size("x"), lax.axis_size("y")
    width = width_all // (n_y * CORES)
    core = lax.axis_index("core")

    slots = n_z * SLOTS
    keep, give, table, mask = attend(
        n_y,
        slots,
        queries,
        new_keys,
        new_values,
        key_cache,
        value_cache,
        lengths,
        resid,
        w_out,
        experts[:, 0],
    )
    given = lax.all_gather(give, "core", axis=0)
    chip = keep + lax.dynamic_index_in_dim(given, 1 - core, 0, keepdims=False)
    chip = chip.astype(bf16).reshape(count, n_y, width)
    packed = jnp.einsum("sr,ryc->ysc", table, chip, preferred_element_type=f32)
    packed = packed.astype(bf16).reshape(n_y * n_z, SLOTS, width)
    got = lax.all_to_all(packed, ("y", "z"), split_axis=0, concat_axis=0, tiled=True)
    hidden = jnp.sum(got.reshape(n_y, slots, width).astype(f32), axis=0)

    spread = jnp.broadcast_to(hidden.astype(bf16)[None], (n_y * n_x, slots, width))
    plane = lax.all_to_all(spread, ("y", "x"), split_axis=0, concat_axis=0, tiled=True)
    pair = lax.all_gather(plane, "core", axis=0)
    keep, give = run_expert(n_x, n_y, pair, norm_gain, w_up[0], w_down[0])
    given = lax.all_gather(give, "core", axis=0)
    half = keep + lax.dynamic_index_in_dim(given, 1 - core, 0, keepdims=False).astype(f32)
    half = half.astype(bf16)
    parts = lax.all_to_all(half, ("y", "x"), split_axis=0, concat_axis=0, tiled=True)
    mixed = (hidden + jnp.sum(parts.astype(f32), axis=0)).astype(bf16)
    back = lax.all_to_all(
        mixed.reshape(n_z, SLOTS, width), "z", split_axis=0, concat_axis=0, tiled=True
    )
    back = back.reshape(slots, 1, width).astype(f32)
    return jnp.sum(mask[:, :, None] * back, axis=0).astype(bf16)


def solution(mesh):
    n_x = GROUP
    n_z = mesh.shape["dp"] // n_x
    n_y = mesh.shape["cuts"] // CORES
    fine = Mesh(mesh.devices.reshape(n_z, n_x, n_y, CORES), ("z", "x", "y", "core"))
    rows, cols = ("z", "x"), ("y", "core")
    placed = (
        P(rows, cols),
        P(rows, cols),
        P(rows, cols),
        P(rows, None, cols),
        P(rows, None, cols),
        P(rows),
        P(rows, None),
        P(),
        P(cols, None),
        P(rows, None),
        P(rows, None, cols),
        P(rows, cols, None),
    )
    return jax.shard_map(
        on_device, mesh=fine, in_specs=placed, out_specs=P(rows, cols), check_vma=False
    )
```

```python
import functools

import jax
import jax.numpy as jnp
from jax import lax
from jax.experimental import pallas as pl
from jax.experimental.pallas import tpu as pltpu
from jax.sharding import Mesh
from jax.sharding import PartitionSpec as P

HD = 128
GROUP = 4
CORES = 2
SLOTS = 2


def in_vmem(shape, dtype):
    return pltpu.VMEM(shape, dtype)


def attend_kernel(n_y, *refs):
    f32, bf16 = jnp.float32, jnp.bfloat16
    sources, (keep, give, table, mask), held, sems = refs[:9], refs[9:13], refs[13:22], refs[22]
    core, my_y = lax.axis_index("core"), lax.axis_index("y")
    copies = [
        pltpu.make_async_copy(source, target, sems.at[i])
        for i, (source, target) in enumerate(zip(sources, held))
    ]
    for copy in copies:
        copy.start()
    lengths, ids, queries, key_cache, new_keys, value_cache, new_values, w_out, resid = held
    count, feats = queries.shape
    spots = key_cache.shape[0]
    length = spots // count
    scale = 1.0 / HD**0.5
    for copy in copies[:2]:
        copy.wait()
    row = lax.broadcasted_iota(jnp.int32, (count, spots), 0)
    spot = lax.broadcasted_iota(jnp.int32, (count, spots), 1)
    limit = jnp.zeros((count, spots), jnp.int32)
    for r in range(count):
        limit = jnp.where(row == r, r * length + lengths[r], limit)
    valid = (spot >= row * length) & (spot < limit)
    slot = lax.broadcasted_iota(jnp.int32, table.shape, 0)
    name = lax.broadcasted_iota(jnp.int32, table.shape, 1)
    hot = jnp.zeros(table.shape, f32)
    for r in range(count):
        place = ids[r] * SLOTS
        for q in range(r):
            place = place + (ids[q] == ids[r]).astype(jnp.int32)
        hot = jnp.where((name == r) & (slot == place), 1.0, hot)
    table[...] = hot.astype(bf16)
    mask[...] = hot
    for copy in copies[2:5]:
        copy.wait()
    probs = []
    for h in range(feats // HD):
        cols = slice(h * HD, (h + 1) * HD)
        query = queries[:, cols]
        scores = lax.dot_general(
            query, key_cache[:, cols], (((1,), (1,)), ((), ())), preferred_element_type=f32
        )
        scores = jnp.where(valid, scores * scale, -1e30)
        fresh = query.astype(f32) * new_keys[:, cols].astype(f32)
        fresh = jnp.sum(fresh, axis=-1, keepdims=True) * scale
        peak = jnp.maximum(jnp.max(scores, axis=-1, keepdims=True), fresh)
        pcache = jnp.where(valid, jnp.exp(scores - peak), 0.0)
        pnew = jnp.exp(fresh - peak)
        total = jnp.sum(pcache, axis=-1, keepdims=True) + pnew
        probs.append(((pcache / total).astype(bf16), (pnew / total).astype(bf16).astype(f32)))
    for copy in copies[5:7]:
        copy.wait()
    heads = []
    for h, (pcache, pnew) in enumerate(probs):
        cols = slice(h * HD, (h + 1) * HD)
        summed = jnp.dot(pcache, value_cache[:, cols], preferred_element_type=f32)
        summed = summed + pnew * new_values[:, cols].astype(f32)
        heads.append(summed.astype(bf16))
    heads_out = jnp.concatenate(heads, axis=1)
    for copy in copies[7:]:
        copy.wait()
    width = w_out.shape[1] // (n_y * CORES)
    for y in range(n_y):
        pair = []
        for c in range(CORES):
            cols = pl.ds((y * CORES + c) * width, width)
            pair.append(jnp.dot(heads_out, w_out[:, cols], preferred_element_type=f32))
        low = resid[:, pl.ds(y * CORES * width, width)].astype(f32)
        high = resid[:, pl.ds((y * CORES + 1) * width, width)].astype(f32)
        rest = jnp.where(my_y == y, jnp.where(core == 0, low, high), 0.0)
        keep[:, pl.ds(y * width, width)] = jnp.where(core == 0, pair[0], pair[1]) + rest
        give[:, pl.ds(y * width, width)] = jnp.where(core == 0, pair[1], pair[0])


def attend(
    n_y,
    slots,
    queries,
    new_keys,
    new_values,
    key_cache,
    value_cache,
    lengths,
    resid,
    w_out,
    ids,
):
    count, feats = queries.shape
    spots = count * key_cache.shape[1]
    args = (
        lengths,
        ids,
        queries,
        key_cache.reshape(spots, feats),
        new_keys,
        value_cache.reshape(spots, feats),
        new_values,
        w_out,
        resid,
    )
    half = in_vmem((count, w_out.shape[1] // CORES), jnp.float32)
    vmem, anywhere = pl.BlockSpec(memory_space=pltpu.VMEM), pl.BlockSpec(memory_space=pl.ANY)
    spaces = [pltpu.SMEM] * 2 + [pltpu.VMEM] * 7
    return pl.pallas_call(
        functools.partial(attend_kernel, n_y),
        out_shape=(
            half,
            half,
            in_vmem((slots, count), jnp.bfloat16),
            in_vmem((slots, count), jnp.float32),
        ),
        in_specs=[anywhere] * len(args),
        out_specs=(vmem,) * 4,
        scratch_shapes=[space(arg.shape, arg.dtype) for space, arg in zip(spaces, args)]
        + [pltpu.SemaphoreType.DMA((len(args),))],
        name="attend",
    )(*args)


def expert_kernel(n_x, n_y, pair, gain, up, down, keep, give):
    f32, bf16 = jnp.float32, jnp.bfloat16
    core = lax.axis_index("core")
    slots, width = pair.shape[2:]
    width_all = n_y * CORES * width
    rows = n_x * slots
    squares = jnp.zeros((rows, width), f32)
    units = jnp.zeros((rows, up.shape[1]), f32)
    for y in range(n_y):
        for c in range(CORES):
            cols = pl.ds((y * CORES + c) * width, width)
            block = [pair[c, x * n_y + y] for x in range(n_x)]
            block = jnp.concatenate(block, axis=0).astype(f32)
            squares = squares + block * block
            scaled = (block * gain[:, cols]).astype(bf16)
            units = units + jnp.dot(scaled, up[cols, :], preferred_element_type=f32)
    meansq = jnp.sum(squares, axis=-1, keepdims=True) * (1.0 / width_all)
    units = units * lax.rsqrt(meansq + 1e-06)
    act = jax.nn.gelu(units).astype(bf16)
    for y in range(n_y):
        both = []
        for c in range(CORES):
            cols = pl.ds((y * CORES + c) * width, width)
            both.append(jnp.dot(act, down[:, cols], preferred_element_type=f32))
        own = jnp.where(core == 0, both[0], both[1])
        other = jnp.where(core == 0, both[1], both[0]).astype(bf16)
        for x in range(n_x):
            keep[y * n_x + x] = own[x * slots : (x + 1) * slots]
            give[y * n_x + x] = other[x * slots : (x + 1) * slots]


def run_expert(n_x, n_y, pair, norm_gain, w_up, w_down):
    vmem = pl.BlockSpec(memory_space=pltpu.VMEM)
    args = [
        pltpu.with_memory_space_constraint(arg, pltpu.VMEM)
        for arg in (pair, norm_gain[None, :], w_up, w_down)
    ]
    return pl.pallas_call(
        functools.partial(expert_kernel, n_x, n_y),
        out_shape=(
            in_vmem(pair.shape[1:], jnp.float32),
            in_vmem(pair.shape[1:], jnp.bfloat16),
        ),
        in_specs=[vmem] * 4,
        out_specs=(vmem, vmem),
        name="expert",
    )(*args)


def on_device(
    queries,
    new_keys,
    new_values,
    key_cache,
    value_cache,
    lengths,
    resid,
    norm_gain,
    w_out,
    experts,
    w_up,
    w_down,
):
    bf16, f32 = jnp.bfloat16, jnp.float32
    count, width_all = resid.shape
    n_z, n_x, n_y = lax.axis_size("z"), lax.axis_size("x"), lax.axis_size("y")
    width = width_all // (n_y * CORES)
    core = lax.axis_index("core")

    slots = n_z * SLOTS
    keep, give, table, mask = attend(
        n_y,
        slots,
        queries,
        new_keys,
        new_values,
        key_cache,
        value_cache,
        lengths,
        resid,
        w_out,
        experts[:, 0],
    )
    given = lax.all_gather(give, "core", axis=0)
    chip = keep + lax.dynamic_index_in_dim(given, 1 - core, 0, keepdims=False)
    chip = chip.astype(bf16).reshape(count, n_y, width)
    packed = jnp.einsum("sr,ryc->ysc", table, chip, preferred_element_type=f32)
    packed = packed.astype(bf16).reshape(n_y * n_z, SLOTS, width)
    got = lax.all_to_all(packed, ("y", "z"), split_axis=0, concat_axis=0, tiled=True)
    hidden = jnp.sum(got.reshape(n_y, slots, width).astype(f32), axis=0)

    spread = jnp.broadcast_to(hidden.astype(bf16)[None], (n_x * n_y, slots, width))
    plane = lax.all_to_all(spread, ("x", "y"), split_axis=0, concat_axis=0, tiled=True)
    pair = lax.all_gather(plane, "core", axis=0)
    keep, give = run_expert(n_x, n_y, pair, norm_gain, w_up[0], w_down[0])
    given = lax.all_gather(give, "core", axis=0)
    half = keep + lax.dynamic_index_in_dim(given, 1 - core, 0, keepdims=False).astype(f32)
    half = half.astype(bf16)
    parts = lax.all_to_all(half, ("y", "x"), split_axis=0, concat_axis=0, tiled=True)
    mixed = (hidden + jnp.sum(parts.astype(f32), axis=0)).astype(bf16)
    back = lax.all_to_all(
        mixed.reshape(n_z, SLOTS, width), "z", split_axis=0, concat_axis=0, tiled=True
    )
    back = back.reshape(slots, 1, width).astype(f32)
    return jnp.sum(mask[:, :, None] * back, axis=0).astype(bf16)


def solution(mesh):
    n_x = GROUP
    n_z = mesh.shape["dp"] // n_x
    n_y = mesh.shape["cuts"] // CORES
    fine = Mesh(mesh.devices.reshape(n_z, n_x, n_y, CORES), ("z", "x", "y", "core"))
    rows, cols = ("z", "x"), ("y", "core")
    placed = (
        P(rows, cols),
        P(rows, cols),
        P(rows, cols),
        P(rows, None, cols),
        P(rows, None, cols),
        P(rows),
        P(rows, None),
        P(),
        P(cols, None),
        P(rows, None),
        P(rows, None, cols),
        P(rows, cols, None),
    )
    return jax.shard_map(
        on_device, mesh=fine, in_specs=placed, out_specs=P(rows, cols), check_vma=False
    )
```

```python
import functools

import jax
import jax.numpy as jnp
from jax import lax
from jax.experimental import pallas as pl
from jax.experimental.pallas import tpu as pltpu
from jax.sharding import Mesh
from jax.sharding import PartitionSpec as P

HD = 128
GROUP = 4
CORES = 2
SLOTS = 2


def in_vmem(shape, dtype):
    return pltpu.VMEM(shape, dtype)


def attend_kernel(n_y, *refs):
    f32, bf16 = jnp.float32, jnp.bfloat16
    sources, (keep, give, table, mask), held, sems = refs[:9], refs[9:13], refs[13:22], refs[22]
    core, my_y = lax.axis_index("core"), lax.axis_index("y")
    copies = [
        pltpu.make_async_copy(source, target, sems.at[i])
        for i, (source, target) in enumerate(zip(sources, held))
    ]
    for copy in copies:
        copy.start()
    lengths, ids, queries, key_cache, new_keys, value_cache, new_values, w_out, resid = held
    count, feats = queries.shape
    spots = key_cache.shape[0]
    length = spots // count
    scale = 1.0 / HD**0.5
    for copy in copies[:2]:
        copy.wait()
    row = lax.broadcasted_iota(jnp.int32, (count, spots), 0)
    spot = lax.broadcasted_iota(jnp.int32, (count, spots), 1)
    limit = jnp.zeros((count, spots), jnp.int32)
    for r in range(count):
        limit = jnp.where(row == r, r * length + lengths[r], limit)
    valid = (spot >= row * length) & (spot < limit)
    slot = lax.broadcasted_iota(jnp.int32, table.shape, 0)
    name = lax.broadcasted_iota(jnp.int32, table.shape, 1)
    hot = jnp.zeros(table.shape, f32)
    for r in range(count):
        place = ids[r] * SLOTS
        for q in range(r):
            place = place + (ids[q] == ids[r]).astype(jnp.int32)
        hot = jnp.where((name == r) & (slot == place), 1.0, hot)
    table[...] = hot.astype(bf16)
    mask[...] = hot
    for copy in copies[2:5]:
        copy.wait()
    probs = []
    for h in range(feats // HD):
        cols = slice(h * HD, (h + 1) * HD)
        query = queries[:, cols]
        scores = lax.dot_general(
            query, key_cache[:, cols], (((1,), (1,)), ((), ())), preferred_element_type=f32
        )
        scores = jnp.where(valid, scores * scale, -1e30)
        fresh = query.astype(f32) * new_keys[:, cols].astype(f32)
        fresh = jnp.sum(fresh, axis=-1, keepdims=True) * scale
        peak = jnp.maximum(jnp.max(scores, axis=-1, keepdims=True), fresh)
        pcache = jnp.where(valid, jnp.exp(scores - peak), 0.0)
        pnew = jnp.exp(fresh - peak)
        total = jnp.sum(pcache, axis=-1, keepdims=True) + pnew
        probs.append(((pcache / total).astype(bf16), (pnew / total).astype(bf16).astype(f32)))
    for copy in copies[5:7]:
        copy.wait()
    heads = []
    for h, (pcache, pnew) in enumerate(probs):
        cols = slice(h * HD, (h + 1) * HD)
        summed = jnp.dot(pcache, value_cache[:, cols], preferred_element_type=f32)
        summed = summed + pnew * new_values[:, cols].astype(f32)
        heads.append(summed.astype(bf16))
    heads_out = jnp.concatenate(heads, axis=1)
    for copy in copies[7:]:
        copy.wait()
    width = w_out.shape[1] // (n_y * CORES)
    for y in range(n_y):
        pair = []
        for c in range(CORES):
            cols = pl.ds((y * CORES + c) * width, width)
            pair.append(jnp.dot(heads_out, w_out[:, cols], preferred_element_type=f32))
        low = resid[:, pl.ds(y * CORES * width, width)].astype(f32)
        high = resid[:, pl.ds((y * CORES + 1) * width, width)].astype(f32)
        rest = jnp.where(my_y == y, jnp.where(core == 0, low, high), 0.0)
        keep[:, pl.ds(y * width, width)] = jnp.where(core == 0, pair[0], pair[1]) + rest
        given = jnp.where(core == 0, pair[1], pair[0])
        give[:, pl.ds(y * width, width)] = given.astype(bf16)


def attend(
    n_y,
    slots,
    queries,
    new_keys,
    new_values,
    key_cache,
    value_cache,
    lengths,
    resid,
    w_out,
    ids,
):
    count, feats = queries.shape
    spots = count * key_cache.shape[1]
    args = (
        lengths,
        ids,
        queries,
        key_cache.reshape(spots, feats),
        new_keys,
        value_cache.reshape(spots, feats),
        new_values,
        w_out,
        resid,
    )
    shape = (count, w_out.shape[1] // CORES)
    vmem, anywhere = pl.BlockSpec(memory_space=pltpu.VMEM), pl.BlockSpec(memory_space=pl.ANY)
    spaces = [pltpu.SMEM] * 2 + [pltpu.VMEM] * 7
    return pl.pallas_call(
        functools.partial(attend_kernel, n_y),
        out_shape=(
            in_vmem(shape, jnp.float32),
            in_vmem(shape, jnp.bfloat16),
            in_vmem((slots, count), jnp.bfloat16),
            in_vmem((slots, count), jnp.float32),
        ),
        in_specs=[anywhere] * len(args),
        out_specs=(vmem,) * 4,
        scratch_shapes=[space(arg.shape, arg.dtype) for space, arg in zip(spaces, args)]
        + [pltpu.SemaphoreType.DMA((len(args),))],
        name="attend",
    )(*args)


def expert_kernel(n_x, n_y, pair, gain, up, down, keep, give):
    f32, bf16 = jnp.float32, jnp.bfloat16
    core = lax.axis_index("core")
    slots, width = pair.shape[2:]
    width_all = n_y * CORES * width
    rows = n_x * slots
    squares = jnp.zeros((rows, width), f32)
    units = jnp.zeros((rows, up.shape[1]), f32)
    for y in range(n_y):
        for c in range(CORES):
            cols = pl.ds((y * CORES + c) * width, width)
            block = [pair[c, y * n_x + x] for x in range(n_x)]
            block = jnp.concatenate(block, axis=0).astype(f32)
            squares = squares + block * block
            scaled = (block * gain[:, cols]).astype(bf16)
            units = units + jnp.dot(scaled, up[cols, :], preferred_element_type=f32)
    meansq = jnp.sum(squares, axis=-1, keepdims=True) * (1.0 / width_all)
    units = units * lax.rsqrt(meansq + 1e-06)
    act = jax.nn.gelu(units).astype(bf16)
    for y in range(n_y):
        both = []
        for c in range(CORES):
            cols = pl.ds((y * CORES + c) * width, width)
            both.append(jnp.dot(act, down[:, cols], preferred_element_type=f32))
        own = jnp.where(core == 0, both[0], both[1])
        other = jnp.where(core == 0, both[1], both[0]).astype(bf16)
        for x in range(n_x):
            keep[y * n_x + x] = own[x * slots : (x + 1) * slots]
            give[y * n_x + x] = other[x * slots : (x + 1) * slots]


def run_expert(n_x, n_y, pair, norm_gain, w_up, w_down):
    vmem = pl.BlockSpec(memory_space=pltpu.VMEM)
    args = [
        pltpu.with_memory_space_constraint(arg, pltpu.VMEM)
        for arg in (pair, norm_gain[None, :], w_up, w_down)
    ]
    return pl.pallas_call(
        functools.partial(expert_kernel, n_x, n_y),
        out_shape=(
            in_vmem(pair.shape[1:], jnp.float32),
            in_vmem(pair.shape[1:], jnp.bfloat16),
        ),
        in_specs=[vmem] * 4,
        out_specs=(vmem, vmem),
        name="expert",
    )(*args)


def on_device(
    queries,
    new_keys,
    new_values,
    key_cache,
    value_cache,
    lengths,
    resid,
    norm_gain,
    w_out,
    experts,
    w_up,
    w_down,
):
    bf16, f32 = jnp.bfloat16, jnp.float32
    count, width_all = resid.shape
    n_z, n_x, n_y = lax.axis_size("z"), lax.axis_size("x"), lax.axis_size("y")
    width = width_all // (n_y * CORES)
    core = lax.axis_index("core")

    slots = n_z * SLOTS
    keep, give, table, mask = attend(
        n_y,
        slots,
        queries,
        new_keys,
        new_values,
        key_cache,
        value_cache,
        lengths,
        resid,
        w_out,
        experts[:, 0],
    )
    given = lax.all_gather(give, "core", axis=0)
    chip = keep + lax.dynamic_index_in_dim(given, 1 - core, 0, keepdims=False).astype(f32)
    chip = chip.astype(bf16).reshape(count, n_y, width)
    packed = jnp.einsum("sr,ryc->ysc", table, chip, preferred_element_type=f32)
    packed = packed.astype(bf16).reshape(n_y * n_z, SLOTS, width)
    got = lax.all_to_all(packed, ("y", "z"), split_axis=0, concat_axis=0, tiled=True)
    hidden = jnp.sum(got.reshape(n_y, slots, width).astype(f32), axis=0)

    spread = jnp.broadcast_to(hidden.astype(bf16)[None], (n_y * n_x, slots, width))
    plane = lax.all_to_all(spread, ("y", "x"), split_axis=0, concat_axis=0, tiled=True)
    pair = lax.all_gather(plane, "core", axis=0)
    keep, give = run_expert(n_x, n_y, pair, norm_gain, w_up[0], w_down[0])
    given = lax.all_gather(give, "core", axis=0)
    half = keep + lax.dynamic_index_in_dim(given, 1 - core, 0, keepdims=False).astype(f32)
    half = half.astype(bf16)
    parts = lax.all_to_all(half, ("y", "x"), split_axis=0, concat_axis=0, tiled=True)
    mixed = (hidden + jnp.sum(parts.astype(f32), axis=0)).astype(bf16)
    back = lax.all_to_all(
        mixed.reshape(n_z, SLOTS, width), "z", split_axis=0, concat_axis=0, tiled=True
    )
    back = back.reshape(slots, 1, width).astype(f32)
    return jnp.sum(mask[:, :, None] * back, axis=0).astype(bf16)


def solution(mesh):
    n_x = GROUP
    n_z = mesh.shape["dp"] // n_x
    n_y = mesh.shape["cuts"] // CORES
    fine = Mesh(mesh.devices.reshape(n_z, n_x, n_y, CORES), ("z", "x", "y", "core"))
    rows, cols = ("z", "x"), ("y", "core")
    placed = (
        P(rows, cols),
        P(rows, cols),
        P(rows, cols),
        P(rows, None, cols),
        P(rows, None, cols),
        P(rows),
        P(rows, None),
        P(),
        P(cols, None),
        P(rows, None),
        P(rows, None, cols),
        P(rows, cols, None),
    )
    return jax.shard_map(
        on_device, mesh=fine, in_specs=placed, out_specs=P(rows, cols), check_vma=False
    )
```

```python
import functools

import jax
import jax.numpy as jnp
from jax import lax
from jax.experimental import pallas as pl
from jax.experimental.pallas import tpu as pltpu
from jax.sharding import Mesh
from jax.sharding import PartitionSpec as P

HD = 128
GROUP = 4
CORES = 2
SLOTS = 2


def in_vmem(shape, dtype):
    return pltpu.VMEM(shape, dtype)


def attend_kernel(n_y, *refs):
    f32, bf16 = jnp.float32, jnp.bfloat16
    sources, (keep, give, table, mask), held, sems = refs[:9], refs[9:13], refs[13:22], refs[22]
    core, my_y = lax.axis_index("core"), lax.axis_index("y")
    copies = [
        pltpu.make_async_copy(source, target, sems.at[i])
        for i, (source, target) in enumerate(zip(sources, held))
    ]
    for copy in copies:
        copy.start()
    lengths, ids, queries, key_cache, new_keys, value_cache, new_values, w_out, resid = held
    count, feats = queries.shape
    spots = key_cache.shape[0]
    length = spots // count
    scale = 1.0 / HD**0.5
    for copy in copies[:2]:
        copy.wait()
    row = lax.broadcasted_iota(jnp.int32, (count, spots), 0)
    spot = lax.broadcasted_iota(jnp.int32, (count, spots), 1)
    limit = jnp.zeros((count, spots), jnp.int32)
    for r in range(count):
        limit = jnp.where(row == r, r * length + lengths[r], limit)
    valid = (spot >= row * length) & (spot < limit)
    slot = lax.broadcasted_iota(jnp.int32, table.shape, 0)
    name = lax.broadcasted_iota(jnp.int32, table.shape, 1)
    hot = jnp.zeros(table.shape, f32)
    for r in range(count):
        place = ids[r] * SLOTS
        for q in range(r):
            place = place + (ids[q] == ids[r]).astype(jnp.int32)
        hot = jnp.where((name == r) & (slot == place), 1.0, hot)
    table[...] = hot.astype(bf16)
    mask[...] = hot
    for copy in copies[2:5]:
        copy.wait()
    probs = []
    for h in range(feats // HD):
        cols = slice(h * HD, (h + 1) * HD)
        query = queries[:, cols]
        scores = lax.dot_general(
            query, key_cache[:, cols], (((1,), (1,)), ((), ())), preferred_element_type=f32
        )
        scores = jnp.where(valid, scores * scale, -1e30)
        fresh = query.astype(f32) * new_keys[:, cols].astype(f32)
        fresh = jnp.sum(fresh, axis=-1, keepdims=True) * scale
        peak = jnp.maximum(jnp.max(scores, axis=-1, keepdims=True), fresh)
        pcache = jnp.where(valid, jnp.exp(scores - peak), 0.0)
        pnew = jnp.exp(fresh - peak)
        total = jnp.sum(pcache, axis=-1, keepdims=True) + pnew
        probs.append(((pcache / total).astype(bf16), (pnew / total).astype(bf16).astype(f32)))
    for copy in copies[5:7]:
        copy.wait()
    heads = []
    for h, (pcache, pnew) in enumerate(probs):
        cols = slice(h * HD, (h + 1) * HD)
        summed = jnp.dot(pcache, value_cache[:, cols], preferred_element_type=f32)
        summed = summed + pnew * new_values[:, cols].astype(f32)
        heads.append(summed.astype(bf16))
    heads_out = jnp.concatenate(heads, axis=1)
    for copy in copies[7:]:
        copy.wait()
    width = w_out.shape[1] // (n_y * CORES)
    for y in range(n_y):
        pair = []
        for c in range(CORES):
            cols = pl.ds((y * CORES + c) * width, width)
            pair.append(jnp.dot(heads_out, w_out[:, cols], preferred_element_type=f32))
        low = resid[:, pl.ds(y * CORES * width, width)].astype(f32)
        high = resid[:, pl.ds((y * CORES + 1) * width, width)].astype(f32)
        rest = jnp.where(my_y == y, jnp.where(core == 0, low, high), 0.0)
        keep[:, pl.ds(y * width, width)] = jnp.where(core == 0, pair[0], pair[1]) + rest
        give[:, pl.ds(y * width, width)] = jnp.where(core == 0, pair[1], pair[0])


def attend(
    n_y,
    slots,
    queries,
    new_keys,
    new_values,
    key_cache,
    value_cache,
    lengths,
    resid,
    w_out,
    ids,
):
    count, feats = queries.shape
    spots = count * key_cache.shape[1]
    args = (
        lengths,
        ids,
        queries,
        key_cache.reshape(spots, feats),
        new_keys,
        value_cache.reshape(spots, feats),
        new_values,
        w_out,
        resid,
    )
    half = in_vmem((count, w_out.shape[1] // CORES), jnp.float32)
    vmem, anywhere = pl.BlockSpec(memory_space=pltpu.VMEM), pl.BlockSpec(memory_space=pl.ANY)
    spaces = [pltpu.SMEM] * 2 + [pltpu.VMEM] * 7
    return pl.pallas_call(
        functools.partial(attend_kernel, n_y),
        out_shape=(
            half,
            half,
            in_vmem((slots, count), jnp.bfloat16),
            in_vmem((slots, count), jnp.float32),
        ),
        in_specs=[anywhere] * len(args),
        out_specs=(vmem,) * 4,
        scratch_shapes=[space(arg.shape, arg.dtype) for space, arg in zip(spaces, args)]
        + [pltpu.SemaphoreType.DMA((len(args),))],
        name="attend",
    )(*args)


def expert_kernel(n_x, n_y, pair, gain, up, down, keep, give):
    f32, bf16 = jnp.float32, jnp.bfloat16
    core = lax.axis_index("core")
    slots, width = pair.shape[2:]
    width_all = n_y * CORES * width
    rows = n_x * slots
    squares = jnp.zeros((rows, width), f32)
    units = jnp.zeros((rows, up.shape[1]), f32)
    for y in range(n_y):
        for c in range(CORES):
            cols = pl.ds((y * CORES + c) * width, width)
            block = [pair[c, x * n_y + y] for x in range(n_x)]
            block = jnp.concatenate(block, axis=0).astype(f32)
            squares = squares + block * block
            scaled = (block * gain[:, cols]).astype(bf16)
            units = units + jnp.dot(scaled, up[cols, :], preferred_element_type=f32)
    meansq = jnp.sum(squares, axis=-1, keepdims=True) * (1.0 / width_all)
    units = units * lax.rsqrt(meansq + 1e-06)
    act = jax.nn.gelu(units).astype(bf16)
    for y in range(n_y):
        both = []
        for c in range(CORES):
            cols = pl.ds((y * CORES + c) * width, width)
            both.append(jnp.dot(act, down[:, cols], preferred_element_type=f32))
        own = jnp.where(core == 0, both[0], both[1]).astype(bf16)
        other = jnp.where(core == 0, both[1], both[0]).astype(bf16)
        for x in range(n_x):
            keep[x * n_y + y] = own[x * slots : (x + 1) * slots]
            give[x * n_y + y] = other[x * slots : (x + 1) * slots]


def run_expert(n_x, n_y, pair, norm_gain, w_up, w_down):
    vmem = pl.BlockSpec(memory_space=pltpu.VMEM)
    args = [
        pltpu.with_memory_space_constraint(arg, pltpu.VMEM)
        for arg in (pair, norm_gain[None, :], w_up, w_down)
    ]
    return pl.pallas_call(
        functools.partial(expert_kernel, n_x, n_y),
        out_shape=(
            in_vmem(pair.shape[1:], jnp.bfloat16),
            in_vmem(pair.shape[1:], jnp.bfloat16),
        ),
        in_specs=[vmem] * 4,
        out_specs=(vmem, vmem),
        name="expert",
    )(*args)


def on_device(
    queries,
    new_keys,
    new_values,
    key_cache,
    value_cache,
    lengths,
    resid,
    norm_gain,
    w_out,
    experts,
    w_up,
    w_down,
):
    bf16, f32 = jnp.bfloat16, jnp.float32
    count, width_all = resid.shape
    n_z, n_x, n_y = lax.axis_size("z"), lax.axis_size("x"), lax.axis_size("y")
    width = width_all // (n_y * CORES)
    core = lax.axis_index("core")

    slots = n_z * SLOTS
    keep, give, table, mask = attend(
        n_y,
        slots,
        queries,
        new_keys,
        new_values,
        key_cache,
        value_cache,
        lengths,
        resid,
        w_out,
        experts[:, 0],
    )
    given = lax.all_gather(give, "core", axis=0)
    chip = keep + lax.dynamic_index_in_dim(given, 1 - core, 0, keepdims=False)
    chip = chip.astype(bf16).reshape(count, n_y, width)
    packed = jnp.einsum("sr,ryc->ysc", table, chip, preferred_element_type=f32)
    packed = packed.astype(bf16).reshape(n_y * n_z, SLOTS, width)
    got = lax.all_to_all(packed, ("y", "z"), split_axis=0, concat_axis=0, tiled=True)
    hidden = jnp.sum(got.reshape(n_y, slots, width).astype(f32), axis=0)

    spread = jnp.broadcast_to(hidden.astype(bf16)[None], (n_x * n_y, slots, width))
    plane = lax.all_to_all(spread, ("x", "y"), split_axis=0, concat_axis=0, tiled=True)
    pair = lax.all_gather(plane, "core", axis=0)
    keep, give = run_expert(n_x, n_y, pair, norm_gain, w_up[0], w_down[0])
    given = lax.all_gather(give, "core", axis=0)
    half = lax.dynamic_index_in_dim(given, 1 - core, 0, keepdims=False).astype(f32)
    half = (keep.astype(f32) + half).astype(bf16)
    parts = lax.all_to_all(half, ("x", "y"), split_axis=0, concat_axis=0, tiled=True)
    mixed = (hidden + jnp.sum(parts.astype(f32), axis=0)).astype(bf16)
    back = lax.all_to_all(
        mixed.reshape(n_z, SLOTS, width), "z", split_axis=0, concat_axis=0, tiled=True
    )
    back = back.reshape(slots, 1, width).astype(f32)
    return jnp.sum(mask[:, :, None] * back, axis=0).astype(bf16)


def solution(mesh):
    n_x = GROUP
    n_z = mesh.shape["dp"] // n_x
    n_y = mesh.shape["cuts"] // CORES
    fine = Mesh(mesh.devices.reshape(n_z, n_x, n_y, CORES), ("z", "x", "y", "core"))
    rows, cols = ("z", "x"), ("y", "core")
    placed = (
        P(rows, cols),
        P(rows, cols),
        P(rows, cols),
        P(rows, None, cols),
        P(rows, None, cols),
        P(rows),
        P(rows, None),
        P(),
        P(cols, None),
        P(rows, None),
        P(rows, None, cols),
        P(rows, cols, None),
    )
    return jax.shard_map(
        on_device, mesh=fine, in_specs=placed, out_specs=P(rows, cols), check_vma=False
    )
```
